256 devices in a mesh: space: 32 (over x, y, core), level: 8 (over z).
Axes of the slice: x: 4, y: 4, z: 8, core: 2. Of those that a mesh axis runs over, the one named last changes fastest.
Arguments:
- fields: bfloat16 [8, 16384, 768], P('level', 'space'), may hold values from -16 to 16
- norm_vert: float32 [768], replicated, may hold values from 0.1 to 1.9
- query_vert: bfloat16 [768, 768], replicated, may hold values from -0.21875 to 0.21875
- keys_vert: bfloat16 [768, 768], replicated, may hold values from -0.21875 to 0.21875
- values_vert: bfloat16 [768, 768], replicated, may hold values from -0.21875 to 0.21875
- out_vert: bfloat16 [768, 768], replicated, may hold values from -0.21875 to 0.21875
- level_bias: float32 [12, 8, 8], replicated, may hold values from -3 to 250
- norm_patch: float32 [768], replicated, may hold values from 0.1 to 1.9
- query_patch: bfloat16 [768, 768], replicated, may hold values from -0.21875 to 0.21875
- keys_patch: bfloat16 [768, 768], replicated, may hold values from -0.21875 to 0.21875
- values_patch: bfloat16 [768, 768], replicated, may hold values from -0.21875 to 0.21875
- out_patch: bfloat16 [768, 768], replicated, may hold values from -0.21875 to 0.21875
- patch_bias: float32 [12, 2], replicated, may hold values from -3 to 250
- neighbours: int32 [64, 4], P('space'), may hold values from -1 to 63, as said below
- counts: int32 [64], P('space'), may hold values from 2 to 4, as said below
- cotangent: bfloat16 [8, 16384, 768], P('level', 'space'), may hold values from -0.015625 to 0.015625
Outputs:
- out_fields: bfloat16 [8, 16384, 768], P('level', 'space')
- grad_wo: float32 [768, 768], P('space')
The draws below stay inside these ranges and needn't reach their ends.
Inputs may be any that keep to these rules, and one draw needn't show every extreme that they name: `neighbours`: row p lists distinct patches, at most one from each device of space, held on devices at cycle distance 1 to 2 from the device of patch p (device s of space holds patches s * 2 to (s + 1) * 2 - 1); entries from counts[p] on are -1. `counts`: some patch has 4 neighbours in every draw.
All inputs are finite; a program needn't handle non-finite values.
Results may differ from the reference program's by a relative error of at most 0.025.
Values may be sent and summed in bfloat16 or wider, within the bound.
No kernel may reach another device: no remote copies, remote signals or barrier semaphores. Data moves between devices by JAX's collectives and lax.ppermute only.
A program may use at most 128 MiB of HBM per device.

```python
import jax
import jax.numpy as jnp
from jax import lax

D = 768
H = 12
HD = 64
PATCH = 256
REACH = 2
PAT_DEV = 2
MAXN = 4
LEV = 8
PATCHES = 64
COLS = 16384
N_SPACE = 32


def draw_fields(key, part):
    noise_key = jax.random.fold_in(key, 0)
    sample = jax.random.normal(noise_key, (LEV, COLS, D), jnp.float32)
    return jnp.clip(sample, -16.0, 16.0).astype(jnp.bfloat16)


def draw_level_bias(key, part):
    noise_key = jax.random.fold_in(key, 0)
    sample = jnp.clip(jax.random.normal(noise_key, (H, LEV, LEV), jnp.float32), -3.0, 3.0)
    return sample


def draw_patch_bias(key, part):
    noise_key = jax.random.fold_in(jax.random.fold_in(key, 11), 0)
    sample = jnp.clip(jax.random.normal(noise_key, (H, 2), jnp.float32), -3.0, 3.0)
    return sample


def neighbour_tables(key):
    base_key = jax.random.fold_in(key, 29)
    order_key, count_key, within_key, full_key = jax.random.split(base_key, 4)
    orders = jax.vmap(lambda one_key: jax.random.permutation(one_key, 2 * REACH))(jax.random.split(order_key, PATCHES))
    signed = jnp.where(orders < REACH, orders + 1, REACH - 1 - orders)
    owners = jnp.arange(PATCHES, dtype=jnp.int32) // PAT_DEV
    far_owner = (owners[:, None] + signed) % N_SPACE
    within = jax.random.randint(within_key, (PATCHES, MAXN), 0, PAT_DEV)
    listed = far_owner * PAT_DEV + within
    tallies = jax.random.randint(count_key, (PATCHES,), 2, MAXN + 1)
    full_patch = jax.random.randint(full_key, (), 0, PATCHES)
    tallies = jnp.where(jnp.arange(PATCHES) == full_patch, MAXN, tallies)
    listed = jnp.where(jnp.arange(MAXN)[None, :] < tallies[:, None], listed, -1)
    return (listed.astype(jnp.int32), tallies.astype(jnp.int32))


def draw_neighbours(key, part):
    return neighbour_tables(key)[0]


def draw_counts(key, part):
    return neighbour_tables(key)[1]


def block_scale(key, dims, cuts, low, largest):
    level = 1.0
    for dim, blocks in cuts:
        steps = jax.random.uniform(jax.random.fold_in(jax.random.fold_in(key, 6), dim), (blocks,), jnp.float32, low / len(cuts), largest / len(cuts))
        level = level * jnp.repeat(jnp.exp(steps), dims[dim] // blocks).reshape((-1,) + (1,) * (len(dims) - 1 - dim))
    return level


def centred(own_key, dims, scale, bound, shards=(), kind=jnp.bfloat16):
    entries = jax.random.normal(own_key, dims, jnp.float32) * scale
    if len(shards) > 0:
        entries = block_scale(own_key, dims, shards, -0.22, 0.18) * entries
    return jnp.clip(entries, min=-bound, max=bound).astype(kind)


def setup_inputs(seed: int = 0) -> dict:
    streams_of = jax.random.split(jax.random.key(seed), 17)
    return {
        "fields": draw_fields(jax.random.fold_in(streams_of[16], 71), 0),
        "norm_vert": jnp.clip(1.0 + 0.18 * jax.random.normal(streams_of[1], (D,), jnp.float32), 0.1, 1.9),
        "query_vert": centred(streams_of[2], (D, D), D ** -0.5, 0.21875),
        "keys_vert": centred(streams_of[3], (D, D), D ** -0.5, 0.21875),
        "values_vert": centred(streams_of[4], (D, D), D ** -0.5, 0.21875),
        "out_vert": centred(streams_of[5], (D, D), D ** -0.5, 0.21875),
        "level_bias": draw_level_bias(jax.random.fold_in(streams_of[16], 71), 0),
        "norm_patch": jnp.clip(1.0 + 0.18 * jax.random.normal(streams_of[7], (D,), jnp.float32), 0.1, 1.9),
        "query_patch": centred(streams_of[8], (D, D), D ** -0.5, 0.21875),
        "keys_patch": centred(streams_of[9], (D, D), D ** -0.5, 0.21875),
        "values_patch": centred(streams_of[10], (D, D), D ** -0.5, 0.21875),
        "out_patch": centred(streams_of[11], (D, D), D ** -0.5, 0.21875),
        "patch_bias": draw_patch_bias(jax.random.fold_in(streams_of[16], 71), 0),
        "neighbours": draw_neighbours(jax.random.fold_in(streams_of[16], 71), 0),
        "counts": draw_counts(jax.random.fold_in(streams_of[16], 71), 0),
        "cotangent": centred(streams_of[15], (LEV, COLS, D), (LEV * COLS) ** -0.5, 0.015625, ((0, 8), (1, 32))),
    }


epsilon = 1e-06

def normalize(values, scaling):
    widened = values.astype(jnp.float32)
    mean_square = lax.optimization_barrier(jnp.mean(widened * widened, axis=-1, keepdims=True))
    return (widened * lax.rsqrt(mean_square + epsilon) * scaling).astype(jnp.bfloat16)

def project(inputs, weight):
    return jnp.dot(inputs, weight, preferred_element_type=jnp.float32).astype(jnp.bfloat16)

def vertical_mix(queries, keys_in, values_in, bias_table):
    level_count, columns, features = queries.shape
    query_heads = queries.astype(jnp.float32).reshape(level_count, columns, H, HD)
    key_heads = keys_in.astype(jnp.float32).reshape(keys_in.shape[0], columns, H, HD)
    value_heads = values_in.astype(jnp.float32).reshape(values_in.shape[0], columns, H, HD)
    scores = jnp.einsum('ichd,jchd->hijc', query_heads, key_heads) * HD ** (-0.5) + bias_table[:, :, :, None]
    weights = jax.nn.softmax(scores, axis=2).astype(jnp.bfloat16)
    mixture = jnp.einsum('hijc,jchd->ichd', weights.astype(jnp.float32), value_heads)
    return mixture.astype(jnp.bfloat16).reshape(level_count, columns, features)

def patch_mix(queries, own_keys, nearby, live_count, bias_table):
    features = queries.shape[-1]
    patch_len = own_keys.shape[0]
    keys_all = jnp.concatenate((own_keys[None], nearby), axis=0).reshape(-1, 2 * features)
    query_heads = queries.astype(jnp.float32).reshape(-1, H, HD)
    key_heads = keys_all[:, :features].astype(jnp.float32).reshape(-1, H, HD)
    value_heads = keys_all[:, features:].astype(jnp.float32).reshape(-1, H, HD)
    scores = jnp.einsum('qhd,khd->hqk', query_heads, key_heads) * HD ** (-0.5)
    block_bias = jnp.concatenate((bias_table[:, :1], jnp.broadcast_to(bias_table[:, 1:], (H, nearby.shape[0]))), axis=1)
    scores = scores + jnp.repeat(block_bias, patch_len, axis=1)[:, None, :]
    opened = jnp.repeat(jnp.arange(nearby.shape[0] + 1, dtype=jnp.int32) <= live_count, patch_len)
    scores = jnp.where(opened[None, None, :], scores, -jnp.inf)
    weights = jax.nn.softmax(scores, axis=-1).astype(jnp.bfloat16)
    mixture = jnp.einsum('hqk,khd->qhd', weights.astype(jnp.float32), value_heads)
    return mixture.astype(jnp.bfloat16).reshape(-1, features)

def reference(fields, norm_vert, query_vert, keys_vert, values_vert, out_vert, level_bias, norm_patch, query_patch, keys_patch, values_patch, out_patch, patch_bias, neighbours, counts, cotangent):
    normed = normalize(fields, norm_vert)
    attn_vert = vertical_mix(project(normed, query_vert), project(normed, keys_vert), project(normed, values_vert), level_bias)
    hidden = (fields.astype(jnp.float32) + jnp.dot(attn_vert, out_vert, preferred_element_type=jnp.float32)).astype(jnp.bfloat16)
    normed_patch = normalize(hidden, norm_patch)
    queries = project(normed_patch, query_patch).reshape(LEV, PATCHES, PATCH, D)
    key_values = jnp.concatenate((project(normed_patch, keys_patch), project(normed_patch, values_patch)), axis=-1).reshape(LEV, PATCHES, PATCH, 2 * D)

    def one_patch(patch_index):
        near_ids = jnp.maximum(neighbours[patch_index], 0).astype(jnp.int32)
        nearby = jnp.take(key_values, near_ids, axis=1)
        own_keys = key_values[:, patch_index]
        own_queries = queries[:, patch_index]
        return jax.vmap(patch_mix, in_axes=(0, 0, 0, None, None))(own_queries, own_keys, nearby, counts[patch_index], patch_bias)
    mixture = lax.map(one_patch, jnp.arange(PATCHES, dtype=jnp.int32))
    attn_patch = jnp.moveaxis(mixture, 0, 1).reshape(LEV, COLS, D)
    out_fields = (hidden.astype(jnp.float32) + jnp.dot(attn_patch, out_patch, preferred_element_type=jnp.float32)).astype(jnp.bfloat16)
    grad_wo = lax.dot_general(attn_patch.reshape(-1, D), cotangent.reshape(-1, D), (((0,), (0,)), ((), ())), preferred_element_type=jnp.float32)
    return (out_fields, grad_wo)
```

```python
import functools

import jax
import jax.numpy as jnp
from jax import lax
from jax.experimental import pallas as pl
from jax.experimental.pallas import tpu as pltpu
from jax.sharding import PartitionSpec as P

H = 12
HD = 64
PATCH = 256
PAIRS = H // 2
GROUP = 16
LOG2E = 1.4426950408889634
epsilon = 1e-06
BF = jnp.bfloat16
F32 = jnp.float32
VMEM_BYTES = 24 * 1024 * 1024


def nn(a, b):
    return jnp.dot(a, b, preferred_element_type=F32)


def nt(a, b):
    return lax.dot_general(a, b, (((1,), (1,)), ((), ())), preferred_element_type=F32)


def normalize(values, gain):
    widened = values.astype(F32)
    mean_square = jnp.mean(widened * widened, axis=-1, keepdims=True)
    return (widened * lax.rsqrt(mean_square + epsilon) * gain).astype(BF)


def paired(two_heads):
    zero = jnp.zeros((HD, two_heads.shape[1]), BF)
    top = jnp.concatenate((two_heads[:HD], zero), axis=1)
    low = jnp.concatenate((zero, two_heads[HD:]), axis=1)
    return jnp.concatenate((top, low), axis=0)


def mixed(values, weights):
    ones = jnp.ones((16, values.shape[1]), BF)
    return nn(jnp.concatenate((values, ones), axis=0), weights)


def vertical_kernel(x, gain, wq, wk, wv, wo, bias, out, normed, q, k, v, mix):
    levels, columns, features = x.shape
    tokens = levels * columns
    block = levels * GROUP
    for level in range(levels):
        rows = normalize(x[level], gain[...])
        for part in range(columns // GROUP):
            place = part * block + level * GROUP
            normed[place : place + GROUP] = rows[part * GROUP : (part + 1) * GROUP]
    for start in range(0, tokens, 256):
        piece = normed[start : start + 256]
        q[:, start : start + 256] = (nt(wq[...], piece) * (HD**-0.5 * LOG2E)).astype(BF)
        v[:, start : start + 256] = nt(wv[...], piece).astype(BF)
        k[start : start + 256] = nn(piece, wk[...]).astype(BF)
    for part in range(columns // GROUP):
        span = slice(part * block, (part + 1) * block)
        for pair in range(PAIRS):
            heads = slice(pair * 128, (pair + 1) * 128)
            scores = nn(k[span, heads], paired(q[heads, span])) + bias[pair]
            top = jnp.max(scores, axis=0, keepdims=True)
            weights = jnp.exp2(scores - top).astype(BF)
            for half in range(2):
                head = slice(pair * 128 + half * HD, pair * 128 + half * HD + HD)
                total = mixed(v[head, span], weights[:, half * block : (half + 1) * block])
                mix[head, span] = (total[:HD] / total[HD : HD + 1]).astype(BF)
    for part in range(columns // GROUP):
        span = slice(part * block, (part + 1) * block)
        projected = nn(mix[:, span].T, wo[...])
        for level in range(levels):
            place = slice(part * GROUP, (part + 1) * GROUP)
            out[level, place] = (
                x[level, place].astype(F32) + projected[level * GROUP : (level + 1) * GROUP]
            ).astype(BF)


def attend(pair, own, start, column, first, q, k, v, pbias, acc, top, total, acc_in, top_in, total_in):
    heads = slice(pair * 128, (pair + 1) * 128)
    mine = slice(own * PATCH, (own + 1) * PATCH)
    row = slice(own * PAIRS + pair, own * PAIRS + pair + 1)
    scores = nn(k[pl.ds(start, PATCH), heads], paired(q[heads, mine]))
    lane = lax.broadcasted_iota(jnp.int32, (1, 2 * PATCH), 1)
    bias = jnp.where(lane < PATCH, pbias[2 * pair, column], pbias[2 * pair + 1, column]) * LOG2E
    largest = jnp.max(scores, axis=0, keepdims=True) + bias
    if not first:
        before = top_in[row]
        largest = jnp.maximum(before, largest)
        fade = jnp.exp2(before - largest)
    weights = jnp.exp2(scores - (largest - bias)).astype(BF)
    top[row] = largest
    sums = []
    for half in range(2):
        head = slice(pair * 128 + half * HD, pair * 128 + half * HD + HD)
        part = slice(half * PATCH, (half + 1) * PATCH)
        found = mixed(v[head, pl.ds(start, PATCH)], weights[:, part])
        sums.append(found[HD : HD + 1])
        if first:
            acc[head, mine] = found[:HD]
        else:
            acc[head, mine] = acc_in[head, mine] * fade[:, part] + found[:HD]
    both = jnp.concatenate(sums, axis=1)
    total[row] = both if first else total_in[row] * fade + both


def keys_values(x, gain, wk, wv, k, v, wq=None, q=None):
    for start in range(0, x.shape[0], PATCH):
        span = slice(start, start + PATCH)
        piece = normalize(x[span], gain[...])
        if wq is not None:
            q[:, span] = (nt(wq[...], piece) * (HD**-0.5 * LOG2E)).astype(BF)
        v[:, span] = nt(wv[...], piece).astype(BF)
        k[span] = nn(piece, wk[...]).astype(BF)


def own_kernel(pbias, x, gain, wq, wk, wv, q, acc, top, total, k, v):
    keys_values(x, gain, wk, wv, k, v, wq, q)
    for own in range(2):
        for pair in range(PAIRS):
            attend(pair, own, own * PATCH, 0, True, q, k, v, pbias, acc, top, total, None, None, None)


def arrived_part(source, near, live, pbias, x, gain, wk, wv, q, acc, top, total, k, v):
    keys_values(x, gain, wk, wv, k, v)
    for own in range(2):
        found = jnp.int32(-1)
        for entry in range(near.shape[1]):
            listed = near[own, entry]
            hit = jnp.logical_and(entry < live[own], lax.shift_right_arithmetic(listed, 1) == source[0])
            found = jnp.where(hit, jnp.bitwise_and(listed, 1), found)

        @pl.when(found >= 0)
        def _():
            start = pl.multiple_of(found * PATCH, PATCH)
            for pair in range(PAIRS):
                attend(pair, own, start, 1, False, q, k, v, pbias, acc, top, total, acc, top, total)


def arrived_kernel(source, near, live, pbias, x, gain, wk, wv, q, acc_in, top_in, total_in, acc, top, total, k, v):
    acc[...] = acc_in[...]
    top[...] = top_in[...]
    total[...] = total_in[...]
    arrived_part(source, near, live, pbias, x, gain, wk, wv, q, acc, top, total, k, v)


def last_kernel(
    source, near, live, pbias, x, gain, wk, wv, q, acc_in, top_in, total_in, cot, mix, grad, acc, top, total, k, v
):
    acc[...] = acc_in[...]
    top[...] = top_in[...]
    total[...] = total_in[...]
    arrived_part(source, near, live, pbias, x, gain, wk, wv, q, acc, top, total, k, v)
    for pair in range(PAIRS):
        heads = slice(pair * 128, (pair + 1) * 128)
        for own in range(2):
            mine = slice(own * PATCH, (own + 1) * PATCH)
            inverse = 1.0 / total[own * PAIRS + pair : own * PAIRS + pair + 1]
            for half in range(2):
                head = slice(pair * 128 + half * HD, pair * 128 + half * HD + HD)
                mix[head, mine] = (
                    acc[head, mine] * inverse[:, half * PATCH : (half + 1) * PATCH]
                ).astype(BF)
        grad[heads] = nn(mix[heads], cot[...]).astype(BF)


IN_VMEM = pl.BlockSpec(memory_space=pltpu.VMEM)
IN_SMEM = pl.BlockSpec(memory_space=pltpu.SMEM)


def call(kernel, scalars, arrays, outs, scratch, flops, name):
    shapes = [jax.ShapeDtypeStruct(shape, kind) for shape, kind in outs]
    moved = sum(a.size * a.dtype.itemsize for a in arrays)
    return pl.pallas_call(
        kernel,
        out_shape=shapes,
        in_specs=[IN_SMEM] * len(scalars) + [IN_VMEM] * len(arrays),
        out_specs=[IN_VMEM] * len(outs),
        scratch_shapes=[pltpu.VMEM(shape, kind) for shape, kind in scratch],
        compiler_params=pltpu.CompilerParams(vmem_limit_bytes=VMEM_BYTES),
        cost_estimate=pl.CostEstimate(flops=flops, bytes_accessed=moved, transcendentals=0),
        name=name,
    )(*scalars, *arrays)


def expanded_bias(level_bias):
    heads, levels, _ = level_bias.shape
    same = jnp.eye(GROUP, dtype=bool)[None, :, None, :]
    table = (level_bias * LOG2E).reshape(PAIRS, 2, levels, levels)
    table = table.transpose(0, 3, 1, 2)
    wide = jnp.where(same, table.reshape(PAIRS * levels, 1, 2 * levels, 1), -jnp.inf)
    return wide.reshape(PAIRS, levels * GROUP, 2 * levels * GROUP)


def body(
    fields,
    norm_vert,
    query_vert,
    keys_vert,
    values_vert,
    out_vert,
    level_bias,
    norm_patch,
    query_patch,
    keys_patch,
    values_patch,
    out_patch,
    patch_bias,
    neighbours,
    counts,
    cotangent,
):
    _, columns, features = fields.shape
    levels = lax.axis_size("level")
    devices = lax.axis_size("space")
    place = lax.axis_index("space")
    share = columns // levels
    square = features * features
    tokens_state = [((features, columns), F32), ((2 * PAIRS, 2 * PATCH), F32), ((2 * PAIRS, 2 * PATCH), F32)]
    key_scratch = [((columns, features), BF), ((features, columns), BF)]

    def moved(value, source_of):
        return lax.ppermute(value, "space", [(source_of(d) % devices, d) for d in range(devices)])

    x = lax.all_to_all(fields.reshape(levels, share, features), "level", 0, 0, tiled=True)
    hidden = call(
        vertical_kernel,
        [],
        [x, norm_vert[None], query_vert.T, keys_vert, values_vert.T, out_vert, expanded_bias(level_bias)],
        [((levels, share, features), BF)],
        [((columns, features), BF), ((features, columns), BF), *key_scratch, ((features, columns), BF)],
        8 * columns * square,
        "vertical",
    )[0]
    hidden = lax.all_to_all(hidden, "level", 0, 0, tiled=True).reshape(columns, features)

    def outer(d):
        return d + 2 if d % 2 == 0 else d - 2

    def inner(d):
        return d - 2 if d % 2 == 0 else d + 2

    def twin(d):
        return d ^ 1

    from_outer = moved(hidden, outer)
    from_twin = moved(hidden, twin)
    from_inner = moved(hidden, inner)
    passed_on = moved(from_outer, twin)
    side = 1 - 2 * (place % 2)
    outer_at = (place + 2 * side) % devices
    inner_at = (place - 2 * side) % devices
    twin_at = place + side
    passed_at = (place - side) % devices
    gain = norm_patch[None]
    wv = values_patch.T
    q, acc, top, total = call(
        own_kernel,
        [patch_bias],
        [hidden, gain, query_patch.T, keys_patch, wv],
        [((features, columns), BF), *tokens_state],
        key_scratch,
        8 * columns * square,
        "own",
    )
    state = [acc, top, total]
    for block, at in ((from_twin, twin_at), (from_outer, outer_at), (passed_on, passed_at)):
        state = call(
            arrived_kernel,
            [at[None], neighbours, counts, patch_bias],
            [block, gain, keys_patch, wv, q, *state],
            tokens_state,
            key_scratch,
            6 * columns * square,
            "arrived",
        )
    mix, grad = call(
        last_kernel,
        [inner_at[None], neighbours, counts, patch_bias],
        [from_inner, gain, keys_patch, wv, q, *state, cotangent.reshape(columns, features)],
        [((features, columns), BF), ((features, features), BF)],
        [*tokens_state, *key_scratch],
        8 * columns * square,
        "last",
    )
    pieces = lax.all_to_all(grad.reshape(devices, features // devices, features), "space", 0, 0, tiled=True)
    shares = pieces.astype(F32).sum(axis=0).astype(BF)
    spread = jnp.broadcast_to(shares[None], (levels, *shares.shape))
    grad_wo = lax.all_to_all(spread, "level", 0, 0, tiled=True).astype(F32).sum(axis=0)
    projected = lax.dot_general(mix, out_patch, (((0,), (0,)), ((), ())), preferred_element_type=F32)
    out_fields = (hidden.astype(F32) + projected).astype(BF)
    return (out_fields[None], grad_wo)


def solution(mesh):
    return jax.shard_map(
        body,
        mesh=mesh,
        in_specs=(
            P("level", "space", None),
            *([P()] * 12),
            P("space", None),
            P("space"),
            P("level", "space", None),
        ),
        out_specs=(P("level", "space", None), P("space", None)),
        check_vma=False,
    )
```

```python
import functools

import jax
import jax.numpy as jnp
from jax import lax
from jax.experimental import pallas as pl
from jax.experimental.pallas import tpu as pltpu
from jax.sharding import PartitionSpec as P

H = 12
HD = 64
PATCH = 256
PAIRS = H // 2
GROUP = 16
LOG2E = 1.4426950408889634
epsilon = 1e-06
BF = jnp.bfloat16
F32 = jnp.float32
VMEM_BYTES = 24 * 1024 * 1024
MOST_VMEM = 63 * 1024 * 1024


def nn(a, b):
    return jnp.dot(a, b, preferred_element_type=F32)


def nt(a, b):
    return lax.dot_general(a, b, (((1,), (1,)), ((), ())), preferred_element_type=F32)


def normalize(values, gain):
    widened = values.astype(F32)
    mean_square = jnp.mean(widened * widened, axis=-1, keepdims=True)
    return (widened * lax.rsqrt(mean_square + epsilon) * gain).astype(BF)


def paired(two_heads):
    zero = jnp.zeros((HD, two_heads.shape[1]), BF)
    top = jnp.concatenate((two_heads[:HD], zero), axis=1)
    low = jnp.concatenate((zero, two_heads[HD:]), axis=1)
    return jnp.concatenate((top, low), axis=0)


def mixed(values, weights):
    ones = jnp.ones((16, values.shape[1]), BF)
    return nn(jnp.concatenate((values, ones), axis=0), weights)


def fetched(pairs, arrivals):
    copies = [pltpu.make_async_copy(a, b, arrivals.at[i]) for i, (a, b) in enumerate(pairs)]
    for copy in copies:
        copy.start()
    return copies


def turning_kernel(*refs):
    count = (len(refs) - 4) // 2
    ins, outs = refs[:count], refs[count : 2 * count]
    landed, turned, arrivals, sent = refs[2 * count :]
    copies = fetched([(ins[i], landed.at[i]) for i in range(count)], arrivals)
    stores = []
    for i in range(count):
        copies[i].wait()
        turned[i] = landed[i].T
        stores.append(pltpu.make_async_copy(turned.at[i], outs[i], sent.at[i]))
        stores[i].start()
    for store in stores:
        store.wait()


def vertical_kernel(
    x_in, wq_in, wk_in, wv_in, wo_in, gain, rows_of_bias, out, normed, q, k, v, mix, bias, x, wq, wk, wv, wo, arrivals
):
    levels, columns, features = x.shape
    copies = fetched([(x_in, x), (wq_in, wq), (wk_in, wk), (wv_in, wv), (wo_in, wo)], arrivals)
    tokens = levels * columns
    block = levels * GROUP
    key_column = lax.broadcasted_iota(jnp.int32, (GROUP, 2 * block), 0)
    query_column = lax.broadcasted_iota(jnp.int32, (GROUP, 2 * block), 1) % GROUP
    same = key_column == query_column
    for pair in range(PAIRS):
        for level in range(levels):
            row = rows_of_bias[pair * levels + level : pair * levels + level + 1]
            bias[pair, level * GROUP : (level + 1) * GROUP] = jnp.where(same, row, -jnp.inf)
    copies[0].wait()
    for level in range(levels):
        rows = normalize(x[level], gain[...])
        for part in range(columns // GROUP):
            place = part * block + level * GROUP
            normed[place : place + GROUP] = rows[part * GROUP : (part + 1) * GROUP]
    spans = [slice(start, start + 256) for start in range(0, tokens, 256)]
    copies[1].wait()
    for span in spans:
        q[:, span] = (nt(wq[...], normed[span]) * (HD**-0.5 * LOG2E)).astype(BF)
    copies[2].wait()
    for span in spans:
        k[span] = nn(normed[span], wk[...]).astype(BF)
    copies[3].wait()
    for span in spans:
        v[:, span] = nt(wv[...], normed[span]).astype(BF)
    steps = [(part, pair) for part in range(columns // GROUP) for pair in range(PAIRS)]

    def step_scores(part, pair):
        span, heads = slice(part * block, (part + 1) * block), slice(pair * 128, (pair + 1) * 128)
        return nn(k[span, heads], paired(q[heads, span])) + bias[pair]

    def step_weights(scores, part, pair):
        return jnp.exp2(scores - jnp.max(scores, axis=0, keepdims=True)).astype(BF)

    def step_mix(weights, part, pair):
        span = slice(part * block, (part + 1) * block)
        for half in range(2):
            head = slice(pair * 128 + half * HD, pair * 128 + half * HD + HD)
            total = mixed(v[head, span], weights[:, half * block : (half + 1) * block])
            mix[head, span] = (total[:HD] / total[HD : HD + 1]).astype(BF)

    staged(steps, step_scores, step_weights, step_mix)
    copies[4].wait()
    for part in range(columns // GROUP):
        span = slice(part * block, (part + 1) * block)
        projected = nn(mix[:, span].T, wo[...])
        for level in range(levels):
            place = slice(part * GROUP, (part + 1) * GROUP)
            out[level, place] = (
                x[level, place].astype(F32) + projected[level * GROUP : (level + 1) * GROUP]
            ).astype(BF)


def pair_scores(pair, own, start, barred, q, k):
    heads = slice(pair * 128, (pair + 1) * 128)
    mine = slice(own * PATCH, (own + 1) * PATCH)
    return nn(k[pl.ds(start, PATCH), heads], paired(q[heads, mine]))


def pair_weights(scores, pair, own, start, barred, column, pbias, new, old):
    row = slice(own * PAIRS + pair, own * PAIRS + pair + 1)
    lane = lax.broadcasted_iota(jnp.int32, (1, 2 * PATCH), 1)
    bias = jnp.where(lane < PATCH, pbias[2 * pair, column], pbias[2 * pair + 1, column]) * LOG2E + barred
    largest = jnp.max(scores, axis=0, keepdims=True) + bias
    fade = None
    if old is not None:
        before = old[1][row]
        largest = jnp.maximum(before, largest)
        fade = jnp.exp2(before - largest)
    new[1][row] = largest
    return jnp.exp2(scores - (largest - bias)).astype(BF), fade


def absorb(weights, fade, pair, own, start, barred, v, new, old):
    mine = slice(own * PATCH, (own + 1) * PATCH)
    row = slice(own * PAIRS + pair, own * PAIRS + pair + 1)
    sums = []
    for half in range(2):
        head = slice(pair * 128 + half * HD, pair * 128 + half * HD + HD)
        part = slice(half * PATCH, (half + 1) * PATCH)
        found = mixed(v[head, pl.ds(start, PATCH)], weights[:, part])
        sums.append(found[HD : HD + 1])
        if old is None:
            new[0][head, mine] = found[:HD]
        else:
            new[0][head, mine] = old[0][head, mine] * fade[:, part] + found[:HD]
    both = jnp.concatenate(sums, axis=1)
    new[2][row] = both if old is None else old[2][row] * fade + both


def staged(steps, first, second, third):
    one, two = {}, {}
    for index in range(len(steps) + 2):
        if index < len(steps):
            one[index] = first(*steps[index])
        if 0 <= index - 1 < len(steps):
            two[index - 1] = second(one.pop(index - 1), *steps[index - 1])
        if 0 <= index - 2:
            third(two.pop(index - 2), *steps[index - 2])


def attend(places, column, q, k, v, pbias, new, old):
    staged(
        [(pair, *place) for place in places for pair in range(PAIRS)],
        lambda *step: pair_scores(*step, q, k),
        lambda scores, *step: pair_weights(scores, *step, column, pbias, new, old),
        lambda found, *step: absorb(*found, *step, v, new, old),
    )


def keys_values(x, gain, wk, wv, k, v, wq=None, q=None):
    for start in range(0, x.shape[0], PATCH):
        span = slice(start, start + PATCH)
        piece = normalize(x[span], gain[...])
        if wq is not None:
            q[:, span] = (nt(wq[...], piece) * (HD**-0.5 * LOG2E)).astype(BF)
        v[:, span] = nt(wv[...], piece).astype(BF)
        k[span] = nn(piece, wk[...]).astype(BF)


def own_kernel(pbias, x, wq_in, wk_in, wv_in, gain, q, acc, top, total, wk, wv, k, v, wq, arrivals):
    for copy in fetched([(wq_in, wq), (wk_in, wk), (wv_in, wv)], arrivals):
        copy.wait()
    keys_values(x, gain, wk, wv, k, v, wq, q)
    attend([(0, 0, 0.0), (1, PATCH, 0.0)], 0, q, k, v, pbias, (acc, top, total), None)


def arrived_part(source, near, live, pbias, x, gain, wk, wv, q, acc_in, top_in, total_in, acc, top, total, k, v):
    keys_values(x, gain, wk, wv, k, v)
    places = []
    for own in range(2):
        found = jnp.int32(-1)
        for entry in range(near.shape[1]):
            listed = near[own, entry]
            hit = jnp.logical_and(entry < live[own], lax.shift_right_arithmetic(listed, 1) == source[0])
            found = jnp.where(hit, jnp.bitwise_and(listed, 1), found)
        barred = jnp.where(found >= 0, 0.0, -jnp.inf)
        places.append((own, pl.multiple_of(jnp.maximum(found, 0) * PATCH, PATCH), barred))
    attend(places, 1, q, k, v, pbias, (acc, top, total), (acc_in, top_in, total_in))


def arrived_kernel(source, near, live, pbias, x, gain, wk, wv, q, acc_in, top_in, total_in, acc, top, total, k, v):
    arrived_part(source, near, live, pbias, x, gain, wk, wv, q, acc_in, top_in, total_in, acc, top, total, k, v)


def last_kernel(
    source, near, live, pbias, x, gain, wk, wv, q, acc_in, top_in, total_in, cot_in, mix_out, grad, acc, top, total, k, v,
    mix, cot, sent
):
    fetch = pltpu.make_async_copy(cot_in, cot, sent.at[0])
    fetch.start()
    arrived_part(source, near, live, pbias, x, gain, wk, wv, q, acc_in, top_in, total_in, acc, top, total, k, v)
    for pair in range(PAIRS):
        heads = slice(pair * 128, (pair + 1) * 128)
        for own in range(2):
            mine = slice(own * PATCH, (own + 1) * PATCH)
            inverse = 1.0 / total[own * PAIRS + pair : own * PAIRS + pair + 1]
            for half in range(2):
                head = slice(pair * 128 + half * HD, pair * 128 + half * HD + HD)
                mix[head, mine] = (
                    acc[head, mine] * inverse[:, half * PATCH : (half + 1) * PATCH]
                ).astype(BF)
        if pair == 0:
            fetch.wait()
        grad[heads] = nn(mix[heads], cot[...]).astype(BF)
    store = pltpu.make_async_copy(mix, mix_out, sent.at[1])
    store.start()
    store.wait()


IN_VMEM = pl.BlockSpec(memory_space=pltpu.VMEM)
IN_SMEM = pl.BlockSpec(memory_space=pltpu.SMEM)
IN_HBM = pl.BlockSpec(memory_space=pltpu.HBM)


def turned(*arrays):
    shape = arrays[0].shape
    several = (len(arrays), *shape)
    return pl.pallas_call(
        turning_kernel,
        out_shape=[jax.ShapeDtypeStruct(shape, BF)] * len(arrays),
        in_specs=[IN_HBM] * len(arrays),
        out_specs=[IN_HBM] * len(arrays),
        scratch_shapes=[
            pltpu.VMEM(several, BF),
            pltpu.VMEM(several, BF),
            pltpu.SemaphoreType.DMA((len(arrays),)),
            pltpu.SemaphoreType.DMA((len(arrays),)),
        ],
        compiler_params=pltpu.CompilerParams(vmem_limit_bytes=MOST_VMEM),
        cost_estimate=pl.CostEstimate(flops=0, bytes_accessed=20 * 2**20, transcendentals=0),
        name="turned",
    )(*arrays)


def call(kernel, scalars, arrays, outs, scratch, flops, name, loose_in=(), loose_out=(), vmem=VMEM_BYTES):
    shapes = [jax.ShapeDtypeStruct(shape, kind) for shape, kind in outs]
    moved = sum(a.size * a.dtype.itemsize for a in arrays)
    return pl.pallas_call(
        kernel,
        out_shape=shapes,
        in_specs=[IN_SMEM] * len(scalars) + [IN_HBM if i in loose_in else IN_VMEM for i in range(len(arrays))],
        out_specs=[IN_HBM if i in loose_out else IN_VMEM for i in range(len(outs))],
        scratch_shapes=[pltpu.VMEM(*s) if isinstance(s, tuple) else s for s in scratch],
        compiler_params=pltpu.CompilerParams(vmem_limit_bytes=vmem),
        cost_estimate=pl.CostEstimate(flops=flops, bytes_accessed=moved, transcendentals=0),
        name=name,
    )(*scalars, *arrays)


def expanded_bias(level_bias):
    levels = level_bias.shape[1]
    table = (level_bias * LOG2E).reshape(PAIRS, 2, levels, levels).transpose(0, 3, 1, 2)
    return jnp.repeat(table.reshape(PAIRS * levels, 2 * levels), GROUP, axis=1)


def sizes(columns, features):
    weights = ((features, features), BF)
    turned_tokens = ((features, columns), BF)
    state = [((features, columns), F32), ((2 * PAIRS, 2 * PATCH), F32), ((2 * PAIRS, 2 * PATCH), F32)]
    return weights, turned_tokens, ((columns, features), BF), state, columns * features * features


def run_vertical(x, wq, wk, wv, wo, gain, rows_of_bias):
    levels, share, features = x.shape
    weights, wide, tall, _, work = sizes(levels * share, features)
    return call(
        vertical_kernel,
        [],
        [x, wq, wk, wv, wo, gain, rows_of_bias],
        [(x.shape, BF)],
        [
            tall,
            wide,
            tall,
            wide,
            wide,
            ((PAIRS, levels * GROUP, 2 * levels * GROUP), F32),
            (x.shape, BF),
            *([weights] * 4),
            pltpu.SemaphoreType.DMA((5,)),
        ],
        10 * work,
        "vertical",
        loose_in=range(5),
        vmem=MOST_VMEM,
    )[0]


def run_own(pbias, hidden, wq, wk, wv, gain):
    weights, wide, tall, state, work = sizes(*hidden.shape)
    return call(
        own_kernel,
        [pbias],
        [hidden, wq, wk, wv, gain],
        [wide, *state, weights, weights],
        [tall, wide, weights, pltpu.SemaphoreType.DMA((3,))],
        8 * work,
        "own",
        loose_in=(1, 2, 3),
    )


def run_arrived(at, fixed, block, gain, wk, wv, q, state):
    _, wide, tall, kept, work = sizes(*block.shape)
    return call(
        arrived_kernel,
        [at[None], *fixed],
        [block, gain, wk, wv, q, *state],
        kept,
        [tall, wide],
        6 * work,
        "arrived",
    )


def run_last(at, fixed, block, gain, wk, wv, q, state, cotangent):
    weights, wide, tall, kept, work = sizes(*block.shape)
    return call(
        last_kernel,
        [at[None], *fixed],
        [block, gain, wk, wv, q, *state, cotangent],
        [wide, weights],
        [*kept, tall, wide, wide, tall, pltpu.SemaphoreType.DMA((2,))],
        8 * work,
        "last",
        loose_in=(8,),
        loose_out=(0,),
    )


def body(
    fields,
    norm_vert,
    query_vert,
    keys_vert,
    values_vert,
    out_vert,
    level_bias,
    norm_patch,
    query_patch,
    keys_patch,
    values_patch,
    out_patch,
    patch_bias,
    neighbours,
    counts,
    cotangent,
):
    _, columns, features = fields.shape
    levels = lax.axis_size("level")
    devices = lax.axis_size("space")
    place = lax.axis_index("space")
    share = columns // levels

    def moved(value, source_of):
        return lax.ppermute(value, "space", [(source_of(d) % devices, d) for d in range(devices)])

    wq_v, wv_v, wq_p, wv_p = turned(query_vert, values_vert, query_patch, values_patch)
    x = lax.all_to_all(fields.reshape(levels, share, features), "level", 0, 0, tiled=True)
    hidden = run_vertical(x, wq_v, keys_vert, wv_v, out_vert, norm_vert[None], expanded_bias(level_bias))
    hidden = lax.all_to_all(hidden, "level", 0, 0, tiled=True).reshape(columns, features)

    def outer(d):
        return d + 2 if d % 2 == 0 else d - 2

    def inner(d):
        return d - 2 if d % 2 == 0 else d + 2

    def twin(d):
        return d ^ 1

    from_outer = moved(hidden, outer)
    from_twin = moved(hidden, twin)
    from_inner = moved(hidden, inner)
    side = 1 - 2 * (place % 2)
    outer_at = (place + 2 * side) % devices
    inner_at = (place - 2 * side) % devices
    twin_at = place + side
    passed_at = (place - side) % devices
    gain = norm_patch[None]
    q, *state, wk, wv = run_own(patch_bias, hidden, wq_p, keys_patch, wv_p, gain)
    fixed = [neighbours, counts, patch_bias]
    state = run_arrived(twin_at, fixed, from_twin, gain, wk, wv, q, state)
    from_outer, *state = lax.optimization_barrier((from_outer, *state))
    passed_on = moved(from_outer, twin)
    state = run_arrived(outer_at, fixed, from_outer, gain, wk, wv, q, state)
    state = run_arrived(passed_at, fixed, passed_on, gain, wk, wv, q, state)
    mix, grad = run_last(
        inner_at, fixed, from_inner, gain, wk, wv, q, state, cotangent.reshape(columns, features)
    )
    pieces = lax.all_to_all(grad.reshape(devices, features // devices, features), "space", 0, 0, tiled=True)
    shares = pieces.astype(F32).sum(axis=0).astype(BF)
    spread = jnp.broadcast_to(shares[None], (levels, *shares.shape))
    grad_wo = lax.all_to_all(spread, "level", 0, 0, tiled=True).astype(F32).sum(axis=0)
    projected = lax.dot_general(mix, out_patch, (((0,), (0,)), ((), ())), preferred_element_type=F32)
    out_fields = (hidden.astype(F32) + projected).astype(BF)
    return (out_fields[None], grad_wo)


def solution(mesh):
    return jax.shard_map(
        body,
        mesh=mesh,
        in_specs=(
            P("level", "space", None),
            *([P()] * 12),
            P("space", None),
            P("space"),
            P("level", "space", None),
        ),
        out_specs=(P("level", "space", None), P("space", None)),
        check_vma=False,
    )
```

```python
import functools

import jax
import jax.numpy as jnp
from jax import lax
from jax.experimental import pallas as pl
from jax.experimental.pallas import tpu as pltpu
from jax.sharding import PartitionSpec as P

H = 12
HD = 64
PATCH = 256
PAIRS = H // 2
GROUP = 16
LOG2E = 1.4426950408889634
epsilon = 1e-06
BF = jnp.bfloat16
F32 = jnp.float32
VMEM_BYTES = 24 * 1024 * 1024
MOST_VMEM = 63 * 1024 * 1024


def nn(a, b):
    return jnp.dot(a, b, preferred_element_type=F32)


def nt(a, b):
    return lax.dot_general(a, b, (((1,), (1,)), ((), ())), preferred_element_type=F32)


def normalize(values, gain):
    widened = values.astype(F32)
    mean_square = jnp.mean(widened * widened, axis=-1, keepdims=True)
    return (widened * lax.rsqrt(mean_square + epsilon) * gain).astype(BF)


def paired(two_heads):
    zero = jnp.zeros((HD, two_heads.shape[1]), BF)
    top = jnp.concatenate((two_heads[:HD], zero), axis=1)
    low = jnp.concatenate((zero, two_heads[HD:]), axis=1)
    return jnp.concatenate((top, low), axis=0)


def mixed(values, weights):
    ones = jnp.ones((16, values.shape[1]), BF)
    return nn(jnp.concatenate((values, ones), axis=0), weights)


def fetched(pairs, arrivals):
    copies = [pltpu.make_async_copy(a, b, arrivals.at[i]) for i, (a, b) in enumerate(pairs)]
    for copy in copies:
        copy.start()
    return copies


def turning_kernel(*refs):
    count = (len(refs) - 4) // 2
    ins, outs = refs[:count], refs[count : 2 * count]
    landed, turned, arrivals, sent = refs[2 * count :]
    copies = fetched([(ins[i], landed.at[i]) for i in range(count)], arrivals)
    stores = []
    for i in range(count):
        copies[i].wait()
        turned[i] = landed[i].T
        stores.append(pltpu.make_async_copy(turned.at[i], outs[i], sent.at[i]))
        stores[i].start()
    for store in stores:
        store.wait()


def vertical_kernel(
    x_in, wq_in, wk_in, wv_in, wo_in, gain, rows_of_bias, out, normed, q, k, v, mix, bias, x, wq, wk, wv, wo, arrivals
):
    levels, columns, features = x.shape
    copies = fetched([(x_in, x), (wq_in, wq), (wk_in, wk), (wv_in, wv), (wo_in, wo)], arrivals)
    tokens = levels * columns
    block = levels * GROUP
    key_column = lax.broadcasted_iota(jnp.int32, (GROUP, 2 * block), 0)
    query_column = lax.broadcasted_iota(jnp.int32, (GROUP, 2 * block), 1) % GROUP
    same = key_column == query_column
    for pair in range(PAIRS):
        for level in range(levels):
            row = rows_of_bias[pair * levels + level : pair * levels + level + 1]
            bias[pair, level * GROUP : (level + 1) * GROUP] = jnp.where(same, row, -jnp.inf)
    copies[0].wait()
    for level in range(levels):
        rows = normalize(x[level], gain[...])
        for part in range(columns // GROUP):
            place = part * block + level * GROUP
            normed[place : place + GROUP] = rows[part * GROUP : (part + 1) * GROUP]
    spans = [slice(start, start + 256) for start in range(0, tokens, 256)]
    copies[1].wait()
    for span in spans:
        q[:, span] = (nt(wq[...], normed[span]) * (HD**-0.5 * LOG2E)).astype(BF)
    copies[2].wait()
    for span in spans:
        k[span] = nn(normed[span], wk[...]).astype(BF)
    copies[3].wait()
    for span in spans:
        v[:, span] = nt(wv[...], normed[span]).astype(BF)
    steps = [(part, pair) for part in range(columns // GROUP) for pair in range(PAIRS)]

    def step_scores(part, pair):
        span, heads = slice(part * block, (part + 1) * block), slice(pair * 128, (pair + 1) * 128)
        return nn(k[span, heads], paired(q[heads, span])) + bias[pair]

    def step_weights(scores, part, pair):
        return jnp.exp2(scores - jnp.max(scores, axis=0, keepdims=True)).astype(BF)

    def step_mix(weights, part, pair):
        span = slice(part * block, (part + 1) * block)
        for half in range(2):
            head = slice(pair * 128 + half * HD, pair * 128 + half * HD + HD)
            total = mixed(v[head, span], weights[:, half * block : (half + 1) * block])
            mix[head, span] = (total[:HD] / total[HD : HD + 1]).astype(BF)

    staged(steps, step_scores, step_weights, step_mix)
    copies[4].wait()
    for part in range(columns // GROUP):
        span = slice(part * block, (part + 1) * block)
        projected = nn(mix[:, span].T, wo[...])
        for level in range(levels):
            place = slice(part * GROUP, (part + 1) * GROUP)
            out[level, place] = (
                x[level, place].astype(F32) + projected[level * GROUP : (level + 1) * GROUP]
            ).astype(BF)


def pair_scores(pair, own, start, barred, q, k):
    heads = slice(pair * 128, (pair + 1) * 128)
    mine = slice(own * PATCH, (own + 1) * PATCH)
    return nn(k[pl.ds(start, PATCH), heads], paired(q[heads, mine]))


def pair_weights(scores, pair, own, start, barred, column, pbias, new, old):
    row = slice(own * PAIRS + pair, own * PAIRS + pair + 1)
    lane = lax.broadcasted_iota(jnp.int32, (1, 2 * PATCH), 1)
    bias = jnp.where(lane < PATCH, pbias[2 * pair, column], pbias[2 * pair + 1, column]) * LOG2E + barred
    largest = jnp.max(scores, axis=0, keepdims=True) + bias
    fade = None
    if old is not None:
        before = old[1][row]
        largest = jnp.maximum(before, largest)
        fade = jnp.exp2(before - largest)
    new[1][row] = largest
    return jnp.exp2(scores - (largest - bias)).astype(BF), fade


def absorb(weights, fade, pair, own, start, barred, v, new, old):
    mine = slice(own * PATCH, (own + 1) * PATCH)
    row = slice(own * PAIRS + pair, own * PAIRS + pair + 1)
    sums = []
    for half in range(2):
        head = slice(pair * 128 + half * HD, pair * 128 + half * HD + HD)
        part = slice(half * PATCH, (half + 1) * PATCH)
        found = mixed(v[head, pl.ds(start, PATCH)], weights[:, part])
        sums.append(found[HD : HD + 1])
        if old is None:
            new[0][head, mine] = found[:HD]
        else:
            new[0][head, mine] = old[0][head, mine] * fade[:, part] + found[:HD]
    both = jnp.concatenate(sums, axis=1)
    new[2][row] = both if old is None else old[2][row] * fade + both


def staged(steps, first, second, third):
    one, two = {}, {}
    for index in range(len(steps) + 2):
        if index < len(steps):
            one[index] = first(*steps[index])
        if 0 <= index - 1 < len(steps):
            two[index - 1] = second(one.pop(index - 1), *steps[index - 1])
        if 0 <= index - 2:
            third(two.pop(index - 2), *steps[index - 2])


def attend(places, column, q, k, v, pbias, new, old):
    staged(
        [(pair, *place) for place in places for pair in range(PAIRS)],
        lambda *step: pair_scores(*step, q, k),
        lambda scores, *step: pair_weights(scores, *step, column, pbias, new, old),
        lambda found, *step: absorb(*found, *step, v, new, old),
    )


def keys_values(x, gain, wk, wv, k, v, wq=None, q=None):
    for start in range(0, x.shape[0], PATCH):
        span = slice(start, start + PATCH)
        piece = normalize(x[span], gain[...])
        if wq is not None:
            q[:, span] = (nt(wq[...], piece) * (HD**-0.5 * LOG2E)).astype(BF)
        v[:, span] = nt(wv[...], piece).astype(BF)
        k[span] = nn(piece, wk[...]).astype(BF)


def own_kernel(pbias, x, wq_in, wk_in, wv_in, gain, q, acc, top, total, wk, wv, again, k, v, wq, arrivals):
    *loads, store = fetched([(wq_in, wq), (wk_in, wk), (wv_in, wv), (x, again)], arrivals)
    for copy in loads:
        copy.wait()
    keys_values(x, gain, wk, wv, k, v, wq, q)
    attend([(0, 0, 0.0), (1, PATCH, 0.0)], 0, q, k, v, pbias, (acc, top, total), None)
    store.wait()


def arrived_part(source, near, live, pbias, x, gain, wk, wv, q, acc_in, top_in, total_in, acc, top, total, k, v):
    keys_values(x, gain, wk, wv, k, v)
    places = []
    for own in range(2):
        found = jnp.int32(-1)
        for entry in range(near.shape[1]):
            listed = near[own, entry]
            hit = jnp.logical_and(entry < live[own], lax.shift_right_arithmetic(listed, 1) == source[0])
            found = jnp.where(hit, jnp.bitwise_and(listed, 1), found)
        barred = jnp.where(found >= 0, 0.0, -jnp.inf)
        places.append((own, pl.multiple_of(jnp.maximum(found, 0) * PATCH, PATCH), barred))
    attend(places, 1, q, k, v, pbias, (acc, top, total), (acc_in, top_in, total_in))


def arrived_kernel(source, near, live, pbias, x, gain, wk, wv, q, acc_in, top_in, total_in, after, *rest):
    acc, top, total, mark, k, v = rest
    arrived_part(source, near, live, pbias, x, gain, wk, wv, q, acc_in, top_in, total_in, acc, top, total, k, v)
    mark[...] = total[:8, :128]


def last_kernel(
    source, core, near, live, pbias, x, gain, wk, wv, q, acc_in, top_in, total_in, cot_in, mix_out, keep, give,
    acc, top, total, k, v, mix, cot, sent
):
    fetch = pltpu.make_async_copy(cot_in, cot, sent.at[0])
    fetch.start()
    arrived_part(source, near, live, pbias, x, gain, wk, wv, q, acc_in, top_in, total_in, acc, top, total, k, v)
    for pair in range(PAIRS):
        for own in range(2):
            mine = slice(own * PATCH, (own + 1) * PATCH)
            inverse = 1.0 / total[own * PAIRS + pair : own * PAIRS + pair + 1]
            for half in range(2):
                head = slice(pair * 128 + half * HD, pair * 128 + half * HD + HD)
                mix[head, mine] = (
                    acc[head, mine] * inverse[:, half * PATCH : (half + 1) * PATCH]
                ).astype(BF)
    store = pltpu.make_async_copy(mix, mix_out, sent.at[1])
    store.start()
    fetch.wait()
    chips, rows, _ = keep.shape
    even = core[0] == 0
    for first in range(0, chips, 8):
        span = slice(first * 2 * rows, (first + 8) * 2 * rows)
        grad = nn(mix[span], cot[...])
        for chip in range(8):
            at = chip * 2 * rows
            to_even, to_odd = grad[at : at + rows], grad[at + rows : at + 2 * rows]
            keep[first + chip] = jnp.where(even, to_even, to_odd)
            give[first + chip] = jnp.where(even, to_odd, to_even).astype(BF)
    store.wait()


IN_VMEM = pl.BlockSpec(memory_space=pltpu.VMEM)
IN_SMEM = pl.BlockSpec(memory_space=pltpu.SMEM)
IN_HBM = pl.BlockSpec(memory_space=pltpu.HBM)


def kept_in_hbm(*arrays):
    return [pltpu.with_memory_space_constraint(array, pltpu.HBM) for array in arrays]


def turned(*arrays):
    shape = arrays[0].shape
    several = (len(arrays), *shape)
    return pl.pallas_call(
        turning_kernel,
        out_shape=[jax.ShapeDtypeStruct(shape, BF)] * len(arrays),
        in_specs=[IN_HBM] * len(arrays),
        out_specs=[IN_HBM] * len(arrays),
        scratch_shapes=[
            pltpu.VMEM(several, BF),
            pltpu.VMEM(several, BF),
            pltpu.SemaphoreType.DMA((len(arrays),)),
            pltpu.SemaphoreType.DMA((len(arrays),)),
        ],
        compiler_params=pltpu.CompilerParams(vmem_limit_bytes=MOST_VMEM),
        cost_estimate=pl.CostEstimate(flops=0, bytes_accessed=20 * 2**20, transcendentals=0),
        name="turned",
    )(*arrays)


def call(kernel, scalars, arrays, outs, scratch, flops, name, loose_in=(), loose_out=(), vmem=VMEM_BYTES):
    shapes = [jax.ShapeDtypeStruct(shape, kind) for shape, kind in outs]
    moved = sum(a.size * a.dtype.itemsize for a in arrays)
    return pl.pallas_call(
        kernel,
        out_shape=shapes,
        in_specs=[IN_SMEM] * len(scalars) + [IN_HBM if i in loose_in else IN_VMEM for i in range(len(arrays))],
        out_specs=[IN_HBM if i in loose_out else IN_VMEM for i in range(len(outs))],
        scratch_shapes=[pltpu.VMEM(*s) if isinstance(s, tuple) else s for s in scratch],
        compiler_params=pltpu.CompilerParams(vmem_limit_bytes=vmem),
        cost_estimate=pl.CostEstimate(flops=flops, bytes_accessed=moved, transcendentals=0),
        name=name,
    )(*scalars, *arrays)


def expanded_bias(level_bias):
    levels = level_bias.shape[1]
    table = (level_bias * LOG2E).reshape(PAIRS, 2, levels, levels).transpose(0, 3, 1, 2)
    return jnp.repeat(table.reshape(PAIRS * levels, 2 * levels), GROUP, axis=1)


MARK = ((8, 128), F32)


def sizes(columns, features):
    weights = ((features, features), BF)
    turned_tokens = ((features, columns), BF)
    state = [((features, columns), F32), ((2 * PAIRS, 2 * PATCH), F32), ((2 * PAIRS, 2 * PATCH), F32)]
    return weights, turned_tokens, ((columns, features), BF), state, columns * features * features


def run_vertical(x, wq, wk, wv, wo, gain, rows_of_bias):
    levels, share, features = x.shape
    weights, wide, tall, _, work = sizes(levels * share, features)
    return call(
        vertical_kernel,
        [],
        [x, wq, wk, wv, wo, gain, rows_of_bias],
        [(x.shape, BF)],
        [
            tall,
            wide,
            tall,
            wide,
            wide,
            ((PAIRS, levels * GROUP, 2 * levels * GROUP), F32),
            (x.shape, BF),
            *([weights] * 4),
            pltpu.SemaphoreType.DMA((5,)),
        ],
        10 * work,
        "vertical",
        loose_in=range(5),
    )[0]


def run_own(pbias, hidden, wq, wk, wv, gain):
    weights, wide, tall, state, work = sizes(*hidden.shape)
    return call(
        own_kernel,
        [pbias],
        [hidden, wq, wk, wv, gain],
        [wide, *state, weights, weights, tall],
        [tall, wide, weights, pltpu.SemaphoreType.DMA((4,))],
        8 * work,
        "own",
        loose_in=(1, 2, 3),
        loose_out=(6,),
    )


def run_arrived(at, fixed, block, gain, wk, wv, q, state, after):
    _, wide, tall, kept, work = sizes(*block.shape)
    return call(
        arrived_kernel,
        [at[None], *fixed],
        [block, gain, wk, wv, q, *state, after],
        [*kept, MARK],
        [tall, wide],
        6 * work,
        "arrived",
        loose_in=(8,),
    )


def run_last(at, core, fixed, block, gain, wk, wv, q, state, cotangent):
    chips = lax.axis_size("space") // 2
    rows = block.shape[1] // (2 * chips)
    piece = (chips, rows, block.shape[1])
    _, wide, tall, kept, work = sizes(*block.shape)
    return call(
        last_kernel,
        [at[None], core[None], *fixed],
        [block, gain, wk, wv, q, *state, cotangent],
        [wide, (piece, F32), (piece, BF)],
        [*kept, tall, wide, wide, tall, pltpu.SemaphoreType.DMA((2,))],
        8 * work,
        "last",
        loose_in=(8,),
        loose_out=(0,),
    )


def body(
    fields,
    norm_vert,
    query_vert,
    keys_vert,
    values_vert,
    out_vert,
    level_bias,
    norm_patch,
    query_patch,
    keys_patch,
    values_patch,
    out_patch,
    patch_bias,
    neighbours,
    counts,
    cotangent,
):
    _, columns, features = fields.shape
    levels = lax.axis_size("level")
    devices = lax.axis_size("space")
    place = lax.axis_index("space")
    share = columns // levels

    def moved(value, source_of):
        return lax.ppermute(value, "space", [(source_of(d) % devices, d) for d in range(devices)])

    wq_v, wv_v, wq_p, wv_p = kept_in_hbm(*turned(query_vert, values_vert, query_patch, values_patch))
    keys_vert, out_vert, keys_patch = kept_in_hbm(keys_vert, out_vert, keys_patch)
    x = lax.all_to_all(fields.reshape(levels, share, features), "level", 0, 0, tiled=True)
    (x,) = kept_in_hbm(x)
    hidden = run_vertical(x, wq_v, keys_vert, wv_v, out_vert, norm_vert[None], expanded_bias(level_bias))
    hidden = lax.all_to_all(hidden, "level", 0, 0, tiled=True).reshape(columns, features)

    def outer(d):
        return d + 2 if d % 2 == 0 else d - 2

    def inner(d):
        return d - 2 if d % 2 == 0 else d + 2

    def twin(d):
        return d ^ 1

    from_outer = moved(hidden, outer)
    from_twin = moved(hidden, twin)
    side = 1 - 2 * (place % 2)
    outer_at = (place + 2 * side) % devices
    inner_at = (place - 2 * side) % devices
    twin_at = place + side
    passed_at = (place - side) % devices
    gain = norm_patch[None]
    q, *state, wk, wv, again = run_own(patch_bias, hidden, wq_p, keys_patch, wv_p, gain)
    from_inner = moved(again, inner)
    fixed = [neighbours, counts, patch_bias]
    *state, mark = run_arrived(twin_at, fixed, from_twin, gain, wk, wv, q, state, jnp.zeros(*MARK))
    from_outer, mark = lax.optimization_barrier((from_outer, mark))
    passed_on = moved(from_outer, twin)
    *state, mark = run_arrived(outer_at, fixed, from_outer, gain, wk, wv, q, state, mark)
    *state, _ = run_arrived(passed_at, fixed, passed_on, gain, wk, wv, q, state, mark)
    mix, keep, give = run_last(
        inner_at, place % 2, fixed, from_inner, gain, wk, wv, q, state, *kept_in_hbm(cotangent.reshape(columns, features))
    )
    summed = (keep + moved(give, twin).astype(F32)).astype(BF)
    same_core = [list(range(core, devices, 2)) for core in range(2)]
    pieces = lax.all_to_all(summed, "space", 0, 0, axis_index_groups=same_core, tiled=True)
    shares = pieces.astype(F32).sum(axis=0).astype(BF)
    spread = jnp.broadcast_to(shares[None], (levels, *shares.shape))
    grad_wo = lax.all_to_all(spread, "level", 0, 0, tiled=True).astype(F32).sum(axis=0)
    projected = lax.dot_general(mix, out_patch, (((0,), (0,)), ((), ())), preferred_element_type=F32)
    out_fields = (hidden.astype(F32) + projected).astype(BF)
    return (out_fields[None], grad_wo)


def solution(mesh):
    return jax.shard_map(
        body,
        mesh=mesh,
        in_specs=(
            P("level", "space", None),
            *([P()] * 12),
            P("space", None),
            P("space"),
            P("level", "space", None),
        ),
        out_specs=(P("level", "space", None), P("space", None)),
        check_vma=False,
    )
```

```python
import functools

import jax
import jax.numpy as jnp
from jax import lax
from jax.experimental import pallas as pl
from jax.experimental.pallas import tpu as pltpu
from jax.sharding import PartitionSpec as P

H = 12
HD = 64
PATCH = 256
PAIRS = H // 2
GROUP = 16
LOG2E = 1.4426950408889634
epsilon = 1e-06
BF = jnp.bfloat16
F32 = jnp.float32
VMEM_BYTES = 24 * 1024 * 1024
MOST_VMEM = 63 * 1024 * 1024


def nn(a, b):
    return jnp.dot(a, b, preferred_element_type=F32)


def nt(a, b):
    return lax.dot_general(a, b, (((1,), (1,)), ((), ())), preferred_element_type=F32)


def normalize(values, gain):
    widened = values.astype(F32)
    mean_square = jnp.mean(widened * widened, axis=-1, keepdims=True)
    return (widened * lax.rsqrt(mean_square + epsilon) * gain).astype(BF)


def paired(two_heads):
    zero = jnp.zeros((HD, two_heads.shape[1]), BF)
    top = jnp.concatenate((two_heads[:HD], zero), axis=1)
    low = jnp.concatenate((zero, two_heads[HD:]), axis=1)
    return jnp.concatenate((top, low), axis=0)


def mixed(values, weights):
    ones = jnp.ones((16, values.shape[1]), BF)
    return nn(jnp.concatenate((values, ones), axis=0), weights)


def fetched(pairs, arrivals):
    copies = [pltpu.make_async_copy(a, b, arrivals.at[i]) for i, (a, b) in enumerate(pairs)]
    for copy in copies:
        copy.start()
    return copies


def turning_kernel(*refs):
    count = (len(refs) - 4) // 2
    ins, outs = refs[:count], refs[count : 2 * count]
    landed, turned, arrivals, sent = refs[2 * count :]
    copies = fetched([(ins[i], landed.at[i]) for i in range(count)], arrivals)
    stores = []
    for i in range(count):
        copies[i].wait()
        turned[i] = landed[i].T
        stores.append(pltpu.make_async_copy(turned.at[i], outs[i], sent.at[i]))
        stores[i].start()
    for store in stores:
        store.wait()


def vertical_kernel(
    _, x, wq_in, wk_in, wv_in, wo_in, gain, rows_of_bias, out, normed, q, k, v, mix, bias, wq, wk, wv, wo, arrivals
):
    levels, columns, features = x.shape
    copies = fetched([(wq_in, wq), (wk_in, wk), (wv_in, wv), (wo_in, wo)], arrivals)
    tokens = levels * columns
    block = levels * GROUP
    key_column = lax.broadcasted_iota(jnp.int32, (GROUP, 2 * block), 0)
    query_column = lax.broadcasted_iota(jnp.int32, (GROUP, 2 * block), 1) % GROUP
    same = key_column == query_column
    for pair in range(PAIRS):
        for level in range(levels):
            row = rows_of_bias[pair * levels + level : pair * levels + level + 1]
            bias[pair, level * GROUP : (level + 1) * GROUP] = jnp.where(same, row, -jnp.inf)
    for level in range(levels):
        rows = normalize(x[level], gain[...])
        for part in range(columns // GROUP):
            place = part * block + level * GROUP
            normed[place : place + GROUP] = rows[part * GROUP : (part + 1) * GROUP]
    spans = [slice(start, start + 256) for start in range(0, tokens, 256)]
    copies[0].wait()
    for span in spans:
        q[:, span] = (nt(wq[...], normed[span]) * (HD**-0.5 * LOG2E)).astype(BF)
    copies[1].wait()
    for span in spans:
        k[span] = nn(normed[span], wk[...]).astype(BF)
    copies[2].wait()
    for span in spans:
        v[:, span] = nt(wv[...], normed[span]).astype(BF)
    steps = [(part, pair) for part in range(columns // GROUP) for pair in range(PAIRS)]

    def step_scores(part, pair):
        span, heads = slice(part * block, (part + 1) * block), slice(pair * 128, (pair + 1) * 128)
        return nn(k[span, heads], paired(q[heads, span])) + bias[pair]

    def step_weights(scores, part, pair):
        return jnp.exp2(scores - jnp.max(scores, axis=0, keepdims=True)).astype(BF)

    def step_mix(weights, part, pair):
        span = slice(part * block, (part + 1) * block)
        for half in range(2):
            head = slice(pair * 128 + half * HD, pair * 128 + half * HD + HD)
            total = mixed(v[head, span], weights[:, half * block : (half + 1) * block])
            mix[head, span] = (total[:HD] / total[HD : HD + 1]).astype(BF)

    staged(steps, step_scores, step_weights, step_mix)
    copies[3].wait()
    for part in range(columns // GROUP):
        span = slice(part * block, (part + 1) * block)
        projected = nn(mix[:, span].T, wo[...])
        for level in range(levels):
            place = slice(part * GROUP, (part + 1) * GROUP)
            out[level, place] = (
                x[level, place].astype(F32) + projected[level * GROUP : (level + 1) * GROUP]
            ).astype(BF)


def pair_scores(pair, own, start, barred, q, k):
    heads = slice(pair * 128, (pair + 1) * 128)
    mine = slice(own * PATCH, (own + 1) * PATCH)
    return nn(k[pl.ds(start, PATCH), heads], paired(q[heads, mine]))


def pair_weights(scores, pair, own, start, barred, column, pbias, new, old):
    row = slice(own * PAIRS + pair, own * PAIRS + pair + 1)
    lane = lax.broadcasted_iota(jnp.int32, (1, 2 * PATCH), 1)
    bias = jnp.where(lane < PATCH, pbias[2 * pair, column], pbias[2 * pair + 1, column]) * LOG2E + barred
    largest = jnp.max(scores, axis=0, keepdims=True) + bias
    fade = None
    if old is not None:
        before = old[1][row]
        largest = jnp.maximum(before, largest)
        fade = jnp.exp2(before - largest)
    new[1][row] = largest
    return jnp.exp2(scores - (largest - bias)).astype(BF), fade


def absorb(weights, fade, pair, own, start, barred, v, new, old):
    mine = slice(own * PATCH, (own + 1) * PATCH)
    row = slice(own * PAIRS + pair, own * PAIRS + pair + 1)
    sums = []
    for half in range(2):
        head = slice(pair * 128 + half * HD, pair * 128 + half * HD + HD)
        part = slice(half * PATCH, (half + 1) * PATCH)
        found = mixed(v[head, pl.ds(start, PATCH)], weights[:, part])
        sums.append(found[HD : HD + 1])
        if old is None:
            new[0][head, mine] = found[:HD]
        else:
            new[0][head, mine] = old[0][head, mine] * fade[:, part] + found[:HD]
    both = jnp.concatenate(sums, axis=1)
    new[2][row] = both if old is None else old[2][row] * fade + both


def staged(steps, first, second, third):
    one, two = {}, {}
    for index in range(len(steps) + 2):
        if index < len(steps):
            one[index] = first(*steps[index])
        if 0 <= index - 1 < len(steps):
            two[index - 1] = second(one.pop(index - 1), *steps[index - 1])
        if 0 <= index - 2:
            third(two.pop(index - 2), *steps[index - 2])


def attend(places, column, q, k, v, pbias, new, old):
    staged(
        [(pair, *place) for place in places for pair in range(PAIRS)],
        lambda *step: pair_scores(*step, q, k),
        lambda scores, *step: pair_weights(scores, *step, column, pbias, new, old),
        lambda found, *step: absorb(*found, *step, v, new, old),
    )


def keys_values(x, gain, wk, wv, k, v):
    for start in range(0, x.shape[0], PATCH):
        span = slice(start, start + PATCH)
        piece = normalize(x[span], gain[...])
        v[:, span] = nt(wv[...], piece).astype(BF)
        k[span] = nn(piece, wk[...]).astype(BF)


def own_kernel(pbias, x, wq_in, wk_in, wv_in, gain, q, acc, top, total, wk, wv, again, k, v, wq, normed, arrivals):
    *loads, store = fetched([(wq_in, wq), (wk_in, wk), (wv_in, wv), (x, again)], arrivals)
    spans = [slice(start, start + PATCH) for start in range(0, x.shape[0], PATCH)]
    for span in spans:
        normed[span] = normalize(x[span], gain[...])
    loads[0].wait()
    for span in spans:
        q[:, span] = (nt(wq[...], normed[span]) * (HD**-0.5 * LOG2E)).astype(BF)
    loads[1].wait()
    for span in spans:
        k[span] = nn(normed[span], wk[...]).astype(BF)
    loads[2].wait()
    for span in spans:
        v[:, span] = nt(wv[...], normed[span]).astype(BF)
    attend([(0, 0, 0.0), (1, PATCH, 0.0)], 0, q, k, v, pbias, (acc, top, total), None)
    store.wait()


def arrived_part(distance, devices, place, near, live, pbias, x, gain, wk, wv, q, acc_in, top_in, total_in, acc, top, total, k, v):
    keys_values(x, gain, wk, wv, k, v)
    outwards = 1 - 2 * lax.rem(place[0], 2)
    source = lax.rem(place[0] + distance * outwards + devices, devices)
    places = []
    for own in range(2):
        found = jnp.int32(-1)
        for entry in range(near.shape[1]):
            listed = near[own, entry]
            hit = jnp.logical_and(entry < live[own], lax.shift_right_arithmetic(listed, 1) == source)
            found = jnp.where(hit, jnp.bitwise_and(listed, 1), found)
        barred = jnp.where(found >= 0, 0.0, -jnp.inf)
        places.append((own, pl.multiple_of(jnp.maximum(found, 0) * PATCH, PATCH), barred))
    attend(places, 1, q, k, v, pbias, (acc, top, total), (acc_in, top_in, total_in))


def arrived_kernel(distance, devices, place, near, live, pbias, x, gain, wk, wv, q, acc_in, top_in, total_in, after, *rest):
    acc, top, total, mark, k, v = rest
    old, new = (acc_in, top_in, total_in), (acc, top, total)
    arrived_part(distance, devices, place, near, live, pbias, x, gain, wk, wv, q, *old, *new, k, v)
    mark[...] = total[:8, :128]


def last_kernel(
    distance, devices, place, near, live, pbias, x, gain, wk, wv, q, acc_in, top_in, total_in, cot_in, mix_out, keep, give,
    acc, top, total, k, v, mix, cot, sent
):
    fetch = pltpu.make_async_copy(cot_in, cot, sent.at[0])
    fetch.start()
    old, new = (acc_in, top_in, total_in), (acc, top, total)
    arrived_part(distance, devices, place, near, live, pbias, x, gain, wk, wv, q, *old, *new, k, v)
    for pair in range(PAIRS):
        for own in range(2):
            mine = slice(own * PATCH, (own + 1) * PATCH)
            inverse = 1.0 / total[own * PAIRS + pair : own * PAIRS + pair + 1]
            for half in range(2):
                head = slice(pair * 128 + half * HD, pair * 128 + half * HD + HD)
                mix[head, mine] = (
                    acc[head, mine] * inverse[:, half * PATCH : (half + 1) * PATCH]
                ).astype(BF)
    store = pltpu.make_async_copy(mix, mix_out, sent.at[1])
    store.start()
    fetch.wait()
    chips, rows, _ = keep.shape
    even = lax.rem(place[0], 2) == 0
    for first in range(0, chips, 8):
        span = slice(first * 2 * rows, (first + 8) * 2 * rows)
        grad = nn(mix[span], cot[...])
        for chip in range(8):
            at = chip * 2 * rows
            to_even, to_odd = grad[at : at + rows], grad[at + rows : at + 2 * rows]
            keep[first + chip] = jnp.where(even, to_even, to_odd)
            give[first + chip] = jnp.where(even, to_odd, to_even).astype(BF)
    store.wait()


IN_VMEM = pl.BlockSpec(memory_space=pltpu.VMEM)
IN_SMEM = pl.BlockSpec(memory_space=pltpu.SMEM)
IN_HBM = pl.BlockSpec(memory_space=pltpu.HBM)


def kept_in_hbm(*arrays):
    return [pltpu.with_memory_space_constraint(array, pltpu.HBM) for array in arrays]


def turned(*arrays):
    shape = arrays[0].shape
    several = (len(arrays), *shape)
    return pl.pallas_call(
        turning_kernel,
        out_shape=[jax.ShapeDtypeStruct(shape, BF)] * len(arrays),
        in_specs=[IN_HBM] * len(arrays),
        out_specs=[IN_HBM] * len(arrays),
        scratch_shapes=[
            pltpu.VMEM(several, BF),
            pltpu.VMEM(several, BF),
            pltpu.SemaphoreType.DMA((len(arrays),)),
            pltpu.SemaphoreType.DMA((len(arrays),)),
        ],
        compiler_params=pltpu.CompilerParams(vmem_limit_bytes=MOST_VMEM),
        cost_estimate=pl.CostEstimate(flops=0, bytes_accessed=20 * 2**20, transcendentals=0),
        name="turned",
    )(*arrays)


def call(kernel, scalars, arrays, outs, scratch, flops, name, loose_in=(), loose_out=(), vmem=VMEM_BYTES):
    shapes = [jax.ShapeDtypeStruct(shape, kind) for shape, kind in outs]
    moved = flops // 256
    return pl.pallas_call(
        kernel,
        out_shape=shapes,
        in_specs=[IN_SMEM] * len(scalars) + [IN_HBM if i in loose_in else IN_VMEM for i in range(len(arrays))],
        out_specs=[IN_HBM if i in loose_out else IN_VMEM for i in range(len(outs))],
        scratch_shapes=[pltpu.VMEM(*s) if isinstance(s, tuple) else s for s in scratch],
        compiler_params=pltpu.CompilerParams(vmem_limit_bytes=vmem),
        cost_estimate=pl.CostEstimate(flops=flops, bytes_accessed=moved, transcendentals=0),
        name=name,
    )(*scalars, *arrays)


def expanded_bias(level_bias):
    levels = level_bias.shape[1]
    table = (level_bias * LOG2E).reshape(PAIRS, 2, levels, levels).transpose(0, 3, 1, 2)
    return jnp.repeat(table.reshape(PAIRS * levels, 2 * levels), GROUP, axis=1)


MARK = ((8, 128), F32)


def sizes(columns, features):
    weights = ((features, features), BF)
    turned_tokens = ((features, columns), BF)
    state = [((features, columns), F32), ((2 * PAIRS, 2 * PATCH), F32), ((2 * PAIRS, 2 * PATCH), F32)]
    return weights, turned_tokens, ((columns, features), BF), state, columns * features * features


def run_vertical(place, x, wq, wk, wv, wo, gain, rows_of_bias):
    levels, share, features = x.shape
    weights, wide, tall, _, work = sizes(levels * share, features)
    return call(
        vertical_kernel,
        [place],
        [x, wq, wk, wv, wo, gain, rows_of_bias],
        [(x.shape, BF)],
        [
            tall,
            wide,
            tall,
            wide,
            wide,
            ((PAIRS, levels * GROUP, 2 * levels * GROUP), F32),
            *([weights] * 4),
            pltpu.SemaphoreType.DMA((4,)),
        ],
        10 * work,
        "vertical",
        loose_in=range(1, 5),
    )[0]


def run_own(pbias, hidden, wq, wk, wv, gain):
    weights, wide, tall, state, work = sizes(*hidden.shape)
    return call(
        own_kernel,
        [pbias],
        [hidden, wq, wk, wv, gain],
        [wide, *state, weights, weights, tall],
        [tall, wide, weights, tall, pltpu.SemaphoreType.DMA((4,))],
        8 * work,
        "own",
        loose_in=(1, 2, 3),
        loose_out=(6,),
    )


def run_arrived(distance, devices, fixed, block, gain, wk, wv, q, state, after):
    _, wide, tall, kept, work = sizes(*block.shape)
    return call(
        functools.partial(arrived_kernel, distance, devices),
        fixed,
        [block, gain, wk, wv, q, *state, after],
        [*kept, MARK],
        [tall, wide],
        work // 4,
        "arrived",
        loose_in=(8,),
    )


def run_last(distance, devices, fixed, block, gain, wk, wv, q, state, cotangent):
    chips = devices // 2
    rows = block.shape[1] // (2 * chips)
    piece = (chips, rows, block.shape[1])
    _, wide, tall, kept, work = sizes(*block.shape)
    return call(
        functools.partial(last_kernel, distance, devices),
        fixed,
        [block, gain, wk, wv, q, *state, cotangent],
        [wide, (piece, F32), (piece, BF)],
        [*kept, tall, wide, wide, tall, pltpu.SemaphoreType.DMA((2,))],
        8 * work,
        "last",
        loose_in=(8,),
        loose_out=(0,),
    )


def body(
    fields,
    norm_vert,
    query_vert,
    keys_vert,
    values_vert,
    out_vert,
    level_bias,
    norm_patch,
    query_patch,
    keys_patch,
    values_patch,
    out_patch,
    patch_bias,
    neighbours,
    counts,
    cotangent,
):
    _, columns, features = fields.shape
    levels = lax.axis_size("level")
    devices = lax.axis_size("space")
    place = lax.axis_index("space")[None]
    share = columns // levels

    def moved(value, source_of):
        return lax.ppermute(value, "space", [(source_of(d) % devices, d) for d in range(devices)])

    wq_v, wv_v, wq_p, wv_p = kept_in_hbm(*turned(query_vert, values_vert, query_patch, values_patch))
    keys_vert, out_vert, keys_patch = kept_in_hbm(keys_vert, out_vert, keys_patch)
    x = lax.all_to_all(fields.reshape(levels, share, features), "level", 0, 0, tiled=True)
    hidden = run_vertical(place, x, wq_v, keys_vert, wv_v, out_vert, norm_vert[None], expanded_bias(level_bias))
    hidden = lax.all_to_all(hidden, "level", 0, 0, tiled=True).reshape(columns, features)

    def outer(d):
        return d + 2 if d % 2 == 0 else d - 2

    def inner(d):
        return d - 2 if d % 2 == 0 else d + 2

    def twin(d):
        return d ^ 1

    from_outer = moved(hidden, outer)
    from_twin = moved(hidden, twin)
    gain = norm_patch[None]
    q, *state, wk, wv, again = run_own(patch_bias, hidden, wq_p, keys_patch, wv_p, gain)
    from_inner = moved(again, inner)
    fixed = [place, neighbours, counts, patch_bias]
    *state, mark = run_arrived(1, devices, fixed, from_twin, gain, wk, wv, q, state, jnp.zeros(*MARK))
    from_outer, mark = lax.optimization_barrier((from_outer, mark))
    passed_on = moved(from_outer, twin)
    *state, mark = run_arrived(2, devices, fixed, from_outer, gain, wk, wv, q, state, mark)
    *state, _ = run_arrived(-1, devices, fixed, passed_on, gain, wk, wv, q, state, mark)
    mix, keep, give = run_last(
        -2, devices, fixed, from_inner, gain, wk, wv, q, state, *kept_in_hbm(cotangent.reshape(columns, features))
    )
    received = moved(give, twin)
    projected = lax.dot_general(mix, out_patch, (((0,), (0,)), ((), ())), preferred_element_type=F32)
    out_fields = (hidden.astype(F32) + projected).astype(BF)
    received, out_fields = lax.optimization_barrier((received, out_fields))
    summed = (keep + received.astype(F32)).astype(BF)
    same_core = [list(range(core, devices, 2)) for core in range(2)]
    pieces = lax.all_to_all(summed, "space", 0, 0, axis_index_groups=same_core, tiled=True)
    shares = pieces.astype(F32).sum(axis=0).astype(BF)
    spread = jnp.broadcast_to(shares[None], (levels, *shares.shape))
    grad_wo = lax.all_to_all(spread, "level", 0, 0, tiled=True).astype(F32).sum(axis=0)
    return (out_fields[None], grad_wo)


def solution(mesh):
    return jax.shard_map(
        body,
        mesh=mesh,
        in_specs=(
            P("level", "space", None),
            *([P()] * 12),
            P("space", None),
            P("space"),
            P("level", "space", None),
        ),
        out_specs=(P("level", "space", None), P("space", None)),
        check_vma=False,
    )
```

```python
import functools

import jax
import jax.numpy as jnp
from jax import lax
from jax.experimental import pallas as pl
from jax.experimental.pallas import tpu as pltpu
from jax.sharding import PartitionSpec as P

H = 12
HD = 64
PATCH = 256
PAIRS = H // 2
GROUP = 16
LOG2E = 1.4426950408889634
epsilon = 1e-06
BF = jnp.bfloat16
F32 = jnp.float32
VMEM_BYTES = 24 * 1024 * 1024
MOST_VMEM = 63 * 1024 * 1024


def nn(a, b):
    return jnp.dot(a, b, preferred_element_type=F32)


def nt(a, b):
    return lax.dot_general(a, b, (((1,), (1,)), ((), ())), preferred_element_type=F32)


def normalize(values, gain):
    widened = values.astype(F32)
    mean_square = jnp.mean(widened * widened, axis=-1, keepdims=True)
    return (widened * lax.rsqrt(mean_square + epsilon) * gain).astype(BF)


def paired(two_heads):
    zero = jnp.zeros((HD, two_heads.shape[1]), BF)
    top = jnp.concatenate((two_heads[:HD], zero), axis=1)
    low = jnp.concatenate((zero, two_heads[HD:]), axis=1)
    return jnp.concatenate((top, low), axis=0)


def mixed(values, weights):
    ones = jnp.ones((16, values.shape[1]), BF)
    return nn(jnp.concatenate((values, ones), axis=0), weights)


def fetched(pairs, arrivals):
    copies = [pltpu.make_async_copy(a, b, arrivals.at[i]) for i, (a, b) in enumerate(pairs)]
    for copy in copies:
        copy.start()
    return copies


def turning_kernel(*refs):
    count = (len(refs) - 4) // 2
    ins, outs = refs[:count], refs[count : 2 * count]
    landed, turned, arrivals, sent = refs[2 * count :]
    copies = fetched([(ins[i], landed.at[i]) for i in range(count)], arrivals)
    stores = []
    for i in range(count):
        copies[i].wait()
        turned[i] = landed[i].T
        stores.append(pltpu.make_async_copy(turned.at[i], outs[i], sent.at[i]))
        stores[i].start()
    for store in stores:
        store.wait()


def vertical_kernel(
    _, x, wq_in, wk_in, wv_in, wo_in, gain, rows_of_bias, out, normed, q, k, v, mix, bias, wq, wk, wv, wo, arrivals
):
    levels, columns, features = x.shape
    copies = fetched([(wq_in, wq), (wk_in, wk), (wv_in, wv), (wo_in, wo)], arrivals)
    tokens = levels * columns
    block = levels * GROUP
    key_column = lax.broadcasted_iota(jnp.int32, (GROUP, 2 * block), 0)
    query_column = lax.broadcasted_iota(jnp.int32, (GROUP, 2 * block), 1) % GROUP
    same = key_column == query_column
    for pair in range(PAIRS):
        for level in range(levels):
            row = rows_of_bias[pair * levels + level : pair * levels + level + 1]
            bias[pair, level * GROUP : (level + 1) * GROUP] = jnp.where(same, row, -jnp.inf)
    for level in range(levels):
        rows = normalize(x[level], gain[...])
        for part in range(columns // GROUP):
            place = part * block + level * GROUP
            normed[place : place + GROUP] = rows[part * GROUP : (part + 1) * GROUP]
    spans = [slice(start, start + 256) for start in range(0, tokens, 256)]
    copies[0].wait()
    for span in spans:
        q[:, span] = (nt(wq[...], normed[span]) * (HD**-0.5 * LOG2E)).astype(BF)
    copies[1].wait()
    for span in spans:
        k[span] = nn(normed[span], wk[...]).astype(BF)
    copies[2].wait()
    for span in spans:
        v[:, span] = nt(wv[...], normed[span]).astype(BF)
    steps = [(part, pair) for part in range(columns // GROUP) for pair in range(PAIRS)]

    def step_scores(part, pair):
        span, heads = slice(part * block, (part + 1) * block), slice(pair * 128, (pair + 1) * 128)
        return nn(k[span, heads], paired(q[heads, span])) + bias[pair]

    def step_weights(scores, part, pair):
        return jnp.exp2(scores - jnp.max(scores, axis=0, keepdims=True)).astype(BF)

    def step_mix(weights, part, pair):
        span = slice(part * block, (part + 1) * block)
        for half in range(2):
            head = slice(pair * 128 + half * HD, pair * 128 + half * HD + HD)
            total = mixed(v[head, span], weights[:, half * block : (half + 1) * block])
            mix[head, span] = (total[:HD] / total[HD : HD + 1]).astype(BF)

    staged(steps, step_scores, step_weights, step_mix)
    copies[3].wait()
    for part in range(columns // GROUP):
        span = slice(part * block, (part + 1) * block)
        projected = nn(mix[:, span].T, wo[...])
        for level in range(levels):
            place = slice(part * GROUP, (part + 1) * GROUP)
            out[level, place] = (
                x[level, place].astype(F32) + projected[level * GROUP : (level + 1) * GROUP]
            ).astype(BF)


def pair_scores(pair, own, start, barred, q, k):
    heads = slice(pair * 128, (pair + 1) * 128)
    mine = slice(own * PATCH, (own + 1) * PATCH)
    return nn(k[pl.ds(start, PATCH), heads], paired(q[heads, mine]))


def pair_weights(scores, pair, own, start, barred, column, pbias, new, old):
    row = slice(own * PAIRS + pair, own * PAIRS + pair + 1)
    lane = lax.broadcasted_iota(jnp.int32, (1, 2 * PATCH), 1)
    bias = jnp.where(lane < PATCH, pbias[2 * pair, column], pbias[2 * pair + 1, column]) * LOG2E + barred
    largest = jnp.max(scores, axis=0, keepdims=True) + bias
    fade = None
    if old is not None:
        before = old[1][row]
        largest = jnp.maximum(before, largest)
        fade = jnp.exp2(before - largest)
    new[1][row] = largest
    return jnp.exp2(scores - (largest - bias)).astype(BF), fade


def absorb(weights, fade, pair, own, start, barred, v, new, old):
    mine = slice(own * PATCH, (own + 1) * PATCH)
    row = slice(own * PAIRS + pair, own * PAIRS + pair + 1)
    sums = []
    for half in range(2):
        head = slice(pair * 128 + half * HD, pair * 128 + half * HD + HD)
        part = slice(half * PATCH, (half + 1) * PATCH)
        found = mixed(v[head, pl.ds(start, PATCH)], weights[:, part])
        sums.append(found[HD : HD + 1])
        if old is None:
            new[0][head, mine] = found[:HD]
        else:
            new[0][head, mine] = old[0][head, mine] * fade[:, part] + found[:HD]
    both = jnp.concatenate(sums, axis=1)
    new[2][row] = both if old is None else old[2][row] * fade + both


def staged(steps, first, second, third):
    one, two = {}, {}
    for index in range(len(steps) + 2):
        if index < len(steps):
            one[index] = first(*steps[index])
        if 0 <= index - 1 < len(steps):
            two[index - 1] = second(one.pop(index - 1), *steps[index - 1])
        if 0 <= index - 2:
            third(two.pop(index - 2), *steps[index - 2])


def attend(places, column, q, k, v, pbias, new, old):
    staged(
        [(pair, *place) for place in places for pair in range(PAIRS)],
        lambda *step: pair_scores(*step, q, k),
        lambda scores, *step: pair_weights(scores, *step, column, pbias, new, old),
        lambda found, *step: absorb(*found, *step, v, new, old),
    )


def keys_values(blocks, gain, wk, wv, k, v):
    done = 0
    for block in blocks:
        for start in range(0, block.shape[0], PATCH):
            span = slice(done, done + PATCH)
            piece = normalize(block[start : start + PATCH], gain[...])
            v[:, span] = nt(wv[...], piece).astype(BF)
            k[span] = nn(piece, wk[...]).astype(BF)
            done += PATCH


def own_kernel(pbias, x, wq_in, wk_in, wv_in, gain, q, acc, top, total, wk, wv, again, k, v, wq, normed, arrivals):
    *loads, store = fetched([(wq_in, wq), (wk_in, wk), (wv_in, wv), (x, again)], arrivals)
    spans = [slice(start, start + PATCH) for start in range(0, x.shape[0], PATCH)]
    for span in spans:
        normed[span] = normalize(x[span], gain[...])
    loads[0].wait()
    for span in spans:
        q[:, span] = (nt(wq[...], normed[span]) * (HD**-0.5 * LOG2E)).astype(BF)
    loads[1].wait()
    for span in spans:
        k[span] = nn(normed[span], wk[...]).astype(BF)
    loads[2].wait()
    for span in spans:
        v[:, span] = nt(wv[...], normed[span]).astype(BF)
    attend([(0, 0, 0.0), (1, PATCH, 0.0)], 0, q, k, v, pbias, (acc, top, total), None)
    store.wait()


def arrived_part(distance, devices, place, near, live, pbias, blocks, gain, wk, wv, q, acc_in, top_in, total_in, acc, top, total, k, v):
    keys_values(blocks, gain, wk, wv, k, v)
    outwards = 1 - 2 * lax.rem(place[0], 2)
    source = lax.rem(place[0] + distance * outwards + devices, devices)
    places = []
    for own in range(2):
        found = jnp.int32(-1)
        for entry in range(near.shape[1]):
            listed = near[own, entry]
            hit = jnp.logical_and(entry < live[own], lax.shift_right_arithmetic(listed, 1) == source)
            found = jnp.where(hit, jnp.bitwise_and(listed, 1), found)
        barred = jnp.where(found >= 0, 0.0, -jnp.inf)
        places.append((own, pl.multiple_of(jnp.maximum(found, 0) * PATCH, PATCH), barred))
    attend(places, 1, q, k, v, pbias, (acc, top, total), (acc_in, top_in, total_in))


def arrived_kernel(distance, devices, count, place, near, live, pbias, *refs):
    blocks, (gain, wk, wv, q, *old) = refs[:count], refs[count : count + 7]
    new, (mark, k, v) = refs[count + 8 : count + 11], refs[count + 11 :]
    arrived_part(distance, devices, place, near, live, pbias, blocks, gain, wk, wv, q, *old, *new, k, v)
    mark[...] = new[2][:8, :128]


def last_kernel(
    distance, devices, place, near, live, pbias, x, gain, wk, wv, q, acc_in, top_in, total_in, cot_in, mix_out, keep, give,
    acc, top, total, k, v, mix, cot, sent
):
    fetch = pltpu.make_async_copy(cot_in, cot, sent.at[0])
    fetch.start()
    old, new = (acc_in, top_in, total_in), (acc, top, total)
    arrived_part(distance, devices, place, near, live, pbias, (x,), gain, wk, wv, q, *old, *new, k, v)
    for pair in range(PAIRS):
        for own in range(2):
            mine = slice(own * PATCH, (own + 1) * PATCH)
            inverse = 1.0 / total[own * PAIRS + pair : own * PAIRS + pair + 1]
            for half in range(2):
                head = slice(pair * 128 + half * HD, pair * 128 + half * HD + HD)
                mix[head, mine] = (
                    acc[head, mine] * inverse[:, half * PATCH : (half + 1) * PATCH]
                ).astype(BF)
    store = pltpu.make_async_copy(mix, mix_out, sent.at[1])
    store.start()
    fetch.wait()
    chips, rows, _ = keep.shape
    even = lax.rem(place[0], 2) == 0
    for first in range(0, chips, 8):
        span = slice(first * 2 * rows, (first + 8) * 2 * rows)
        grad = nn(mix[span], cot[...])
        for chip in range(8):
            at = chip * 2 * rows
            to_even, to_odd = grad[at : at + rows], grad[at + rows : at + 2 * rows]
            keep[first + chip] = jnp.where(even, to_even, to_odd)
            give[first + chip] = jnp.where(even, to_odd, to_even).astype(BF)
    store.wait()


IN_VMEM = pl.BlockSpec(memory_space=pltpu.VMEM)
IN_SMEM = pl.BlockSpec(memory_space=pltpu.SMEM)
IN_HBM = pl.BlockSpec(memory_space=pltpu.HBM)


def kept_in_hbm(*arrays):
    return [pltpu.with_memory_space_constraint(array, pltpu.HBM) for array in arrays]


def turned(*arrays):
    shape = arrays[0].shape
    several = (len(arrays), *shape)
    return pl.pallas_call(
        turning_kernel,
        out_shape=[jax.ShapeDtypeStruct(shape, BF)] * len(arrays),
        in_specs=[IN_HBM] * len(arrays),
        out_specs=[IN_HBM] * len(arrays),
        scratch_shapes=[
            pltpu.VMEM(several, BF),
            pltpu.VMEM(several, BF),
            pltpu.SemaphoreType.DMA((len(arrays),)),
            pltpu.SemaphoreType.DMA((len(arrays),)),
        ],
        compiler_params=pltpu.CompilerParams(vmem_limit_bytes=MOST_VMEM),
        cost_estimate=pl.CostEstimate(flops=0, bytes_accessed=20 * 2**20, transcendentals=0),
        name="turned",
    )(*arrays)


def call(kernel, scalars, arrays, outs, scratch, flops, name, loose_in=(), loose_out=(), vmem=VMEM_BYTES):
    shapes = [jax.ShapeDtypeStruct(shape, kind) for shape, kind in outs]
    moved = flops // 256
    return pl.pallas_call(
        kernel,
        out_shape=shapes,
        in_specs=[IN_SMEM] * len(scalars) + [IN_HBM if i in loose_in else IN_VMEM for i in range(len(arrays))],
        out_specs=[IN_HBM if i in loose_out else IN_VMEM for i in range(len(outs))],
        scratch_shapes=[pltpu.VMEM(*s) if isinstance(s, tuple) else s for s in scratch],
        compiler_params=pltpu.CompilerParams(vmem_limit_bytes=vmem),
        cost_estimate=pl.CostEstimate(flops=flops, bytes_accessed=moved, transcendentals=0),
        name=name,
    )(*scalars, *arrays)


def halving_kernel(block, _, first, second, sent):
    rows = first.shape[0]
    for copy in fetched([(block.at[:rows], first), (block.at[rows:], second)], sent):
        copy.wait()


def halved(block, after):
    half = ((block.shape[0] // 2, block.shape[1]), BF)
    return call(
        halving_kernel,
        [],
        [block, after],
        [half, half],
        [pltpu.SemaphoreType.DMA((2,))],
        0,
        "halved",
        loose_in=(0, 1),
        loose_out=(0, 1),
    )


def expanded_bias(level_bias):
    levels = level_bias.shape[1]
    table = (level_bias * LOG2E).reshape(PAIRS, 2, levels, levels).transpose(0, 3, 1, 2)
    return jnp.repeat(table.reshape(PAIRS * levels, 2 * levels), GROUP, axis=1)


MARK = ((8, 128), F32)


def sizes(columns, features):
    weights = ((features, features), BF)
    turned_tokens = ((features, columns), BF)
    state = [((features, columns), F32), ((2 * PAIRS, 2 * PATCH), F32), ((2 * PAIRS, 2 * PATCH), F32)]
    return weights, turned_tokens, ((columns, features), BF), state, columns * features * features


def run_vertical(place, x, wq, wk, wv, wo, gain, rows_of_bias):
    levels, share, features = x.shape
    weights, wide, tall, _, work = sizes(levels * share, features)
    return call(
        vertical_kernel,
        [place],
        [x, wq, wk, wv, wo, gain, rows_of_bias],
        [(x.shape, BF)],
        [
            tall,
            wide,
            tall,
            wide,
            wide,
            ((PAIRS, levels * GROUP, 2 * levels * GROUP), F32),
            *([weights] * 4),
            pltpu.SemaphoreType.DMA((4,)),
        ],
        10 * work,
        "vertical",
        loose_in=range(1, 5),
    )[0]


def run_own(pbias, hidden, wq, wk, wv, gain):
    weights, wide, tall, state, work = sizes(*hidden.shape)
    return call(
        own_kernel,
        [pbias],
        [hidden, wq, wk, wv, gain],
        [wide, *state, weights, weights, tall],
        [tall, wide, weights, tall, pltpu.SemaphoreType.DMA((4,))],
        8 * work,
        "own",
        loose_in=(1, 2, 3),
        loose_out=(6,),
    )


def run_arrived(distance, devices, fixed, blocks, gain, wk, wv, q, state, after):
    _, wide, tall, kept, work = sizes(*q.shape[::-1])
    return call(
        functools.partial(arrived_kernel, distance, devices, len(blocks)),
        fixed,
        [*blocks, gain, wk, wv, q, *state, after],
        [*kept, MARK],
        [tall, wide],
        work // 4,
        "arrived",
        loose_in=(len(blocks) + 7,),
    )


def run_last(distance, devices, fixed, block, gain, wk, wv, q, state, cotangent):
    chips = devices // 2
    rows = block.shape[1] // (2 * chips)
    piece = (chips, rows, block.shape[1])
    _, wide, tall, kept, work = sizes(*block.shape)
    return call(
        functools.partial(last_kernel, distance, devices),
        fixed,
        [block, gain, wk, wv, q, *state, cotangent],
        [wide, (piece, F32), (piece, BF)],
        [*kept, tall, wide, wide, tall, pltpu.SemaphoreType.DMA((2,))],
        8 * work,
        "last",
        loose_in=(8,),
        loose_out=(0,),
    )


def body(
    fields,
    norm_vert,
    query_vert,
    keys_vert,
    values_vert,
    out_vert,
    level_bias,
    norm_patch,
    query_patch,
    keys_patch,
    values_patch,
    out_patch,
    patch_bias,
    neighbours,
    counts,
    cotangent,
):
    _, columns, features = fields.shape
    levels = lax.axis_size("level")
    devices = lax.axis_size("space")
    place = lax.axis_index("space")[None]
    share = columns // levels

    def moved(value, source_of):
        return lax.ppermute(value, "space", [(source_of(d) % devices, d) for d in range(devices)])

    wq_v, wv_v, wq_p, wv_p = kept_in_hbm(*turned(query_vert, values_vert, query_patch, values_patch))
    keys_vert, out_vert, keys_patch = kept_in_hbm(keys_vert, out_vert, keys_patch)
    x = lax.all_to_all(fields.reshape(levels, share, features), "level", 0, 0, tiled=True)
    hidden = run_vertical(place, x, wq_v, keys_vert, wv_v, out_vert, norm_vert[None], expanded_bias(level_bias))
    hidden = lax.all_to_all(hidden, "level", 0, 0, tiled=True).reshape(columns, features)

    def outer(d):
        return d + 2 if d % 2 == 0 else d - 2

    def inner(d):
        return d - 2 if d % 2 == 0 else d + 2

    def twin(d):
        return d ^ 1

    from_outer = moved(hidden, outer)
    from_twin = moved(hidden, twin)
    gain = norm_patch[None]
    q, *state, wk, wv, again = run_own(patch_bias, hidden, wq_p, keys_patch, wv_p, gain)
    from_inner = moved(again, inner)
    fixed = [place, neighbours, counts, patch_bias]
    *state, mark = run_arrived(1, devices, fixed, [from_twin], gain, wk, wv, q, state, jnp.zeros(*MARK))
    passed_on = [moved(half, twin) for half in halved(from_outer, mark)]
    *state, mark = run_arrived(2, devices, fixed, [from_outer], gain, wk, wv, q, state, mark)
    *state, _ = run_arrived(-1, devices, fixed, passed_on, gain, wk, wv, q, state, mark)
    mix, keep, give = run_last(
        -2, devices, fixed, from_inner, gain, wk, wv, q, state, *kept_in_hbm(cotangent.reshape(columns, features))
    )
    received = moved(give, twin)
    projected = lax.dot_general(mix, out_patch, (((0,), (0,)), ((), ())), preferred_element_type=F32)
    out_fields = (hidden.astype(F32) + projected).astype(BF)
    received, out_fields = lax.optimization_barrier((received, out_fields))
    summed = (keep + received.astype(F32)).astype(BF)
    same_core = [list(range(core, devices, 2)) for core in range(2)]
    pieces = lax.all_to_all(summed, "space", 0, 0, axis_index_groups=same_core, tiled=True)
    shares = pieces.astype(F32).sum(axis=0).astype(BF)
    spread = jnp.broadcast_to(shares[None], (levels, *shares.shape))
    grad_wo = lax.all_to_all(spread, "level", 0, 0, tiled=True).astype(F32).sum(axis=0)
    return (out_fields[None], grad_wo)


def solution(mesh):
    return jax.shard_map(
        body,
        mesh=mesh,
        in_specs=(
            P("level", "space", None),
            *([P()] * 12),
            P("space", None),
            P("space"),
            P("level", "space", None),
        ),
        out_specs=(P("level", "space", None), P("space", None)),
        check_vma=False,
    )
```

```python
import functools

import jax
import jax.numpy as jnp
from jax import lax
from jax.experimental import pallas as pl
from jax.experimental.pallas import tpu as pltpu
from jax.sharding import PartitionSpec as P

H = 12
HD = 64
PATCH = 256
PAIRS = H // 2
TEAM = 4
TEAMS = H // TEAM
GROUP = 16
LOG2E = 1.4426950408889634
epsilon = 1e-06
BF = jnp.bfloat16
F32 = jnp.float32
VMEM_BYTES = 24 * 1024 * 1024
MOST_VMEM = 63 * 1024 * 1024


def nn(a, b):
    return jnp.dot(a, b, preferred_element_type=F32)


def nt(a, b):
    return lax.dot_general(a, b, (((1,), (1,)), ((), ())), preferred_element_type=F32)


def normalize(values, gain):
    widened = values.astype(F32)
    mean_square = jnp.mean(widened * widened, axis=-1, keepdims=True)
    return (widened * lax.rsqrt(mean_square + epsilon) * gain).astype(BF)


def paired(queries):
    heads = queries.shape[0] // HD
    zero = jnp.zeros((HD, queries.shape[1]), BF)
    rows = []
    for head in range(heads):
        own = queries[head * HD : (head + 1) * HD]
        rows.append(jnp.concatenate([own if other == head else zero for other in range(heads)], axis=1))
    return jnp.concatenate(rows, axis=0)


def mixed(values, weights):
    ones = jnp.ones((16, values.shape[1]), BF)
    return nn(jnp.concatenate((values, ones), axis=0), weights)


def fetched(pairs, arrivals):
    copies = [pltpu.make_async_copy(a, b, arrivals.at[i]) for i, (a, b) in enumerate(pairs)]
    for copy in copies:
        copy.start()
    return copies


def turning_kernel(*refs):
    count = (len(refs) - 4) // 2
    ins, outs = refs[:count], refs[count : 2 * count]
    landed, turned, arrivals, sent = refs[2 * count :]
    copies = fetched([(ins[i], landed.at[i]) for i in range(count)], arrivals)
    stores = []
    for i in range(count):
        copies[i].wait()
        turned[i] = landed[i].T
        stores.append(pltpu.make_async_copy(turned.at[i], outs[i], sent.at[i]))
        stores[i].start()
    for store in stores:
        store.wait()


def vertical_kernel(
    _, x, wq_in, wk_in, wv_in, wo_in, gain, rows_of_bias, out, normed, q, k, v, mix, bias, wq, wk, wv, wo, arrivals
):
    levels, columns, features = x.shape
    copies = fetched([(wq_in, wq), (wk_in, wk), (wv_in, wv), (wo_in, wo)], arrivals)
    tokens = levels * columns
    block = levels * GROUP
    key_column = lax.broadcasted_iota(jnp.int32, (GROUP, TEAM * block), 0)
    query_column = lax.broadcasted_iota(jnp.int32, (GROUP, TEAM * block), 1) % GROUP
    same = key_column == query_column
    for team in range(TEAMS):
        for level in range(levels):
            row = rows_of_bias[team * levels + level : team * levels + level + 1]
            bias[team, level * GROUP : (level + 1) * GROUP] = jnp.where(same, row, -jnp.inf)
    for level in range(levels):
        rows = normalize(x[level], gain[...])
        for part in range(columns // GROUP):
            place = part * block + level * GROUP
            normed[place : place + GROUP] = rows[part * GROUP : (part + 1) * GROUP]
    spans = [slice(start, start + 256) for start in range(0, tokens, 256)]
    copies[0].wait()
    for span in spans:
        q[:, span] = (nt(wq[...], normed[span]) * (HD**-0.5 * LOG2E)).astype(BF)
    copies[1].wait()
    for span in spans:
        k[span] = nn(normed[span], wk[...]).astype(BF)
    copies[2].wait()
    for span in spans:
        v[:, span] = nt(wv[...], normed[span]).astype(BF)
    steps = [(part, team) for part in range(columns // GROUP) for team in range(TEAMS)]

    def step_scores(part, team):
        span, heads = slice(part * block, (part + 1) * block), slice(team * TEAM * HD, (team + 1) * TEAM * HD)
        return nn(k[span, heads], paired(q[heads, span])) + bias[team]

    def step_weights(scores, part, team):
        return jnp.exp2(scores - jnp.max(scores, axis=0, keepdims=True)).astype(BF)

    def step_mix(weights, part, team):
        span = slice(part * block, (part + 1) * block)
        for half in range(TEAM):
            head = slice((team * TEAM + half) * HD, (team * TEAM + half + 1) * HD)
            total = mixed(v[head, span], weights[:, half * block : (half + 1) * block])
            mix[head, span] = (total[:HD] / total[HD : HD + 1]).astype(BF)

    staged(steps, step_scores, step_weights, step_mix)
    copies[3].wait()
    for part in range(columns // GROUP):
        span = slice(part * block, (part + 1) * block)
        projected = nn(mix[:, span].T, wo[...])
        for level in range(levels):
            place = slice(part * GROUP, (part + 1) * GROUP)
            out[level, place] = (
                x[level, place].astype(F32) + projected[level * GROUP : (level + 1) * GROUP]
            ).astype(BF)


def pair_scores(pair, own, start, barred, q, k):
    heads = slice(pair * 128, (pair + 1) * 128)
    mine = slice(own * PATCH, (own + 1) * PATCH)
    return nn(k[pl.ds(start, PATCH), heads], paired(q[heads, mine]))


def pair_weights(scores, pair, own, start, barred, column, pbias, new, old):
    row = slice(own * PAIRS + pair, own * PAIRS + pair + 1)
    lane = lax.broadcasted_iota(jnp.int32, (1, 2 * PATCH), 1)
    bias = jnp.where(lane < PATCH, pbias[2 * pair, column], pbias[2 * pair + 1, column]) * LOG2E + barred
    largest = jnp.max(scores, axis=0, keepdims=True) + bias
    fade = None
    if old is not None:
        before = old[1][row]
        largest = jnp.maximum(before, largest)
        fade = jnp.exp2(before - largest)
    new[1][row] = largest
    return jnp.exp2(scores - (largest - bias)).astype(BF), fade


def absorb(weights, fade, pair, own, start, barred, v, new, old):
    mine = slice(own * PATCH, (own + 1) * PATCH)
    row = slice(own * PAIRS + pair, own * PAIRS + pair + 1)
    sums = []
    for half in range(2):
        head = slice(pair * 128 + half * HD, pair * 128 + half * HD + HD)
        part = slice(half * PATCH, (half + 1) * PATCH)
        found = mixed(v[head, pl.ds(start, PATCH)], weights[:, part])
        sums.append(found[HD : HD + 1])
        if old is None:
            new[0][head, mine] = found[:HD]
        else:
            new[0][head, mine] = old[0][head, mine] * fade[:, part] + found[:HD]
    both = jnp.concatenate(sums, axis=1)
    new[2][row] = both if old is None else old[2][row] * fade + both


def staged(steps, first, second, third):
    one, two = {}, {}
    for index in range(len(steps) + 2):
        if index < len(steps):
            one[index] = first(*steps[index])
        if 0 <= index - 1 < len(steps):
            two[index - 1] = second(one.pop(index - 1), *steps[index - 1])
        if 0 <= index - 2:
            third(two.pop(index - 2), *steps[index - 2])


def attend(places, column, q, k, v, pbias, new, old):
    staged(
        [(pair, *place) for place in places for pair in range(PAIRS)],
        lambda *step: pair_scores(*step, q, k),
        lambda scores, *step: pair_weights(scores, *step, column, pbias, new, old),
        lambda found, *step: absorb(*found, *step, v, new, old),
    )


def keys_values(blocks, gain, wk, wv, k, v):
    done = 0
    for block in blocks:
        for start in range(0, block.shape[0], PATCH):
            span = slice(done, done + PATCH)
            piece = normalize(block[start : start + PATCH], gain[...])
            v[:, span] = nt(wv[...], piece).astype(BF)
            k[span] = nn(piece, wk[...]).astype(BF)
            done += PATCH


def own_kernel(pbias, x, wq_in, wk_in, wv_in, gain, q, acc, top, total, wk, wv, again, k, v, wq, normed, arrivals):
    *loads, store = fetched([(wq_in, wq), (wk_in, wk), (wv_in, wv), (x, again)], arrivals)
    spans = [slice(start, start + PATCH) for start in range(0, x.shape[0], PATCH)]
    for span in spans:
        normed[span] = normalize(x[span], gain[...])
    loads[0].wait()
    for span in spans:
        q[:, span] = (nt(wq[...], normed[span]) * (HD**-0.5 * LOG2E)).astype(BF)
    loads[1].wait()
    for span in spans:
        k[span] = nn(normed[span], wk[...]).astype(BF)
    loads[2].wait()
    for span in spans:
        v[:, span] = nt(wv[...], normed[span]).astype(BF)
    attend([(0, 0, 0.0), (1, PATCH, 0.0)], 0, q, k, v, pbias, (acc, top, total), None)
    store.wait()


def arrived_part(distance, devices, place, near, live, pbias, blocks, gain, wk, wv, q, acc_in, top_in, total_in, acc, top, total, k, v):
    keys_values(blocks, gain, wk, wv, k, v)
    outwards = 1 - 2 * lax.rem(place[0], 2)
    source = lax.rem(place[0] + distance * outwards + devices, devices)
    places = []
    for own in range(2):
        found = jnp.int32(-1)
        for entry in range(near.shape[1]):
            listed = near[own, entry]
            hit = jnp.logical_and(entry < live[own], lax.shift_right_arithmetic(listed, 1) == source)
            found = jnp.where(hit, jnp.bitwise_and(listed, 1), found)
        barred = jnp.where(found >= 0, 0.0, -jnp.inf)
        places.append((own, pl.multiple_of(jnp.maximum(found, 0) * PATCH, PATCH), barred))
    attend(places, 1, q, k, v, pbias, (acc, top, total), (acc_in, top_in, total_in))


def arrived_kernel(distance, devices, count, place, near, live, pbias, *refs):
    blocks, (gain, wk, wv, q, *old) = refs[:count], refs[count : count + 7]
    new, (mark, k, v) = refs[count + 8 : count + 11], refs[count + 11 :]
    arrived_part(distance, devices, place, near, live, pbias, blocks, gain, wk, wv, q, *old, *new, k, v)
    mark[...] = new[2][:8, :128]


def last_kernel(
    distance, devices, place, near, live, pbias, x, gain, wk, wv, q, acc_in, top_in, total_in, cot_in, mix_out, keep, give,
    acc, top, total, k, v, mix, cot, sent
):
    fetch = pltpu.make_async_copy(cot_in, cot, sent.at[0])
    fetch.start()
    old, new = (acc_in, top_in, total_in), (acc, top, total)
    arrived_part(distance, devices, place, near, live, pbias, (x,), gain, wk, wv, q, *old, *new, k, v)
    for pair in range(PAIRS):
        for own in range(2):
            mine = slice(own * PATCH, (own + 1) * PATCH)
            inverse = 1.0 / total[own * PAIRS + pair : own * PAIRS + pair + 1]
            for half in range(2):
                head = slice(pair * 128 + half * HD, pair * 128 + half * HD + HD)
                mix[head, mine] = (
                    acc[head, mine] * inverse[:, half * PATCH : (half + 1) * PATCH]
                ).astype(BF)
    store = pltpu.make_async_copy(mix, mix_out, sent.at[1])
    store.start()
    fetch.wait()
    chips, rows, _ = keep.shape
    even = lax.rem(place[0], 2) == 0
    for first in range(0, chips, 8):
        span = slice(first * 2 * rows, (first + 8) * 2 * rows)
        grad = nn(mix[span], cot[...])
        for chip in range(8):
            at = chip * 2 * rows
            to_even, to_odd = grad[at : at + rows], grad[at + rows : at + 2 * rows]
            keep[first + chip] = jnp.where(even, to_even, to_odd)
            give[first + chip] = jnp.where(even, to_odd, to_even).astype(BF)
    store.wait()


IN_VMEM = pl.BlockSpec(memory_space=pltpu.VMEM)
IN_SMEM = pl.BlockSpec(memory_space=pltpu.SMEM)
IN_HBM = pl.BlockSpec(memory_space=pltpu.HBM)


def kept_in_hbm(*arrays):
    return [pltpu.with_memory_space_constraint(array, pltpu.HBM) for array in arrays]


def turned(*arrays):
    shape = arrays[0].shape
    several = (len(arrays), *shape)
    return pl.pallas_call(
        turning_kernel,
        out_shape=[jax.ShapeDtypeStruct(shape, BF)] * len(arrays),
        in_specs=[IN_HBM] * len(arrays),
        out_specs=[IN_HBM] * len(arrays),
        scratch_shapes=[
            pltpu.VMEM(several, BF),
            pltpu.VMEM(several, BF),
            pltpu.SemaphoreType.DMA((len(arrays),)),
            pltpu.SemaphoreType.DMA((len(arrays),)),
        ],
        compiler_params=pltpu.CompilerParams(vmem_limit_bytes=MOST_VMEM),
        cost_estimate=pl.CostEstimate(flops=0, bytes_accessed=20 * 2**20, transcendentals=0),
        name="turned",
    )(*arrays)


def call(kernel, scalars, arrays, outs, scratch, flops, name, loose_in=(), loose_out=(), vmem=VMEM_BYTES):
    shapes = [jax.ShapeDtypeStruct(shape, kind) for shape, kind in outs]
    moved = flops // 256
    return pl.pallas_call(
        kernel,
        out_shape=shapes,
        in_specs=[IN_SMEM] * len(scalars) + [IN_HBM if i in loose_in else IN_VMEM for i in range(len(arrays))],
        out_specs=[IN_HBM if i in loose_out else IN_VMEM for i in range(len(outs))],
        scratch_shapes=[pltpu.VMEM(*s) if isinstance(s, tuple) else s for s in scratch],
        compiler_params=pltpu.CompilerParams(vmem_limit_bytes=vmem),
        cost_estimate=pl.CostEstimate(flops=flops, bytes_accessed=moved, transcendentals=0),
        name=name,
    )(*scalars, *arrays)


def halving_kernel(block, _, first, second, sent):
    rows = first.shape[0]
    for copy in fetched([(block.at[:rows], first), (block.at[rows:], second)], sent):
        copy.wait()


def halved(block, after):
    half = ((block.shape[0] // 2, block.shape[1]), BF)
    return call(
        halving_kernel,
        [],
        [block, after],
        [half, half],
        [pltpu.SemaphoreType.DMA((2,))],
        0,
        "halved",
        loose_in=(0, 1),
        loose_out=(0, 1),
    )


def expanded_bias(level_bias):
    levels = level_bias.shape[1]
    table = (level_bias * LOG2E).reshape(TEAMS, TEAM, levels, levels).transpose(0, 3, 1, 2)
    return jnp.repeat(table.reshape(TEAMS * levels, TEAM * levels), GROUP, axis=1)


MARK = ((8, 128), F32)


def sizes(columns, features):
    weights = ((features, features), BF)
    turned_tokens = ((features, columns), BF)
    state = [((features, columns), F32), ((2 * PAIRS, 2 * PATCH), F32), ((2 * PAIRS, 2 * PATCH), F32)]
    return weights, turned_tokens, ((columns, features), BF), state, columns * features * features


def run_vertical(place, x, wq, wk, wv, wo, gain, rows_of_bias):
    levels, share, features = x.shape
    weights, wide, tall, _, work = sizes(levels * share, features)
    return call(
        vertical_kernel,
        [place],
        [x, wq, wk, wv, wo, gain, rows_of_bias],
        [(x.shape, BF)],
        [
            tall,
            wide,
            tall,
            wide,
            wide,
            ((TEAMS, levels * GROUP, TEAM * levels * GROUP), F32),
            *([weights] * 4),
            pltpu.SemaphoreType.DMA((4,)),
        ],
        10 * work,
        "vertical",
        loose_in=range(1, 5),
    )[0]


def run_own(pbias, hidden, wq, wk, wv, gain):
    weights, wide, tall, state, work = sizes(*hidden.shape)
    return call(
        own_kernel,
        [pbias],
        [hidden, wq, wk, wv, gain],
        [wide, *state, weights, weights, tall],
        [tall, wide, weights, tall, pltpu.SemaphoreType.DMA((4,))],
        8 * work,
        "own",
        loose_in=(1, 2, 3),
        loose_out=(6,),
    )


def run_arrived(distance, devices, fixed, blocks, gain, wk, wv, q, state, after):
    _, wide, tall, kept, work = sizes(*q.shape[::-1])
    return call(
        functools.partial(arrived_kernel, distance, devices, len(blocks)),
        fixed,
        [*blocks, gain, wk, wv, q, *state, after],
        [*kept, MARK],
        [tall, wide],
        work // 4,
        "arrived",
        loose_in=(len(blocks) + 7,),
    )


def run_last(distance, devices, fixed, block, gain, wk, wv, q, state, cotangent):
    chips = devices // 2
    rows = block.shape[1] // (2 * chips)
    piece = (chips, rows, block.shape[1])
    _, wide, tall, kept, work = sizes(*block.shape)
    return call(
        functools.partial(last_kernel, distance, devices),
        fixed,
        [block, gain, wk, wv, q, *state, cotangent],
        [wide, (piece, F32), (piece, BF)],
        [*kept, tall, wide, wide, tall, pltpu.SemaphoreType.DMA((2,))],
        8 * work,
        "last",
        loose_in=(8,),
        loose_out=(0,),
    )


def body(
    fields,
    norm_vert,
    query_vert,
    keys_vert,
    values_vert,
    out_vert,
    level_bias,
    norm_patch,
    query_patch,
    keys_patch,
    values_patch,
    out_patch,
    patch_bias,
    neighbours,
    counts,
    cotangent,
):
    _, columns, features = fields.shape
    levels = lax.axis_size("level")
    devices = lax.axis_size("space")
    place = lax.axis_index("space")[None]
    share = columns // levels

    def moved(value, source_of):
        return lax.ppermute(value, "space", [(source_of(d) % devices, d) for d in range(devices)])

    wq_v, wv_v, wq_p, wv_p = kept_in_hbm(*turned(query_vert, values_vert, query_patch, values_patch))
    keys_vert, out_vert, keys_patch = kept_in_hbm(keys_vert, out_vert, keys_patch)
    x = lax.all_to_all(fields.reshape(levels, share, features), "level", 0, 0, tiled=True)
    hidden = run_vertical(place, x, wq_v, keys_vert, wv_v, out_vert, norm_vert[None], expanded_bias(level_bias))
    hidden = lax.all_to_all(hidden, "level", 0, 0, tiled=True).reshape(columns, features)

    def outer(d):
        return d + 2 if d % 2 == 0 else d - 2

    def inner(d):
        return d - 2 if d % 2 == 0 else d + 2

    def twin(d):
        return d ^ 1

    from_outer = moved(hidden, outer)
    from_twin = moved(hidden, twin)
    gain = norm_patch[None]
    q, *state, wk, wv, again = run_own(patch_bias, hidden, wq_p, keys_patch, wv_p, gain)
    from_inner = moved(again, inner)
    fixed = [place, neighbours, counts, patch_bias]
    *state, mark = run_arrived(1, devices, fixed, [from_twin], gain, wk, wv, q, state, jnp.zeros(*MARK))
    passed_on = [moved(half, twin) for half in halved(from_outer, mark)]
    *state, mark = run_arrived(2, devices, fixed, [from_outer], gain, wk, wv, q, state, mark)
    *state, _ = run_arrived(-1, devices, fixed, passed_on, gain, wk, wv, q, state, mark)
    mix, keep, give = run_last(
        -2, devices, fixed, from_inner, gain, wk, wv, q, state, *kept_in_hbm(cotangent.reshape(columns, features))
    )
    received = moved(give, twin)
    projected = lax.dot_general(mix, out_patch, (((0,), (0,)), ((), ())), preferred_element_type=F32)
    out_fields = (hidden.astype(F32) + projected).astype(BF)
    received, out_fields = lax.optimization_barrier((received, out_fields))
    summed = (keep + received.astype(F32)).astype(BF)
    same_core = [list(range(core, devices, 2)) for core in range(2)]
    pieces = lax.all_to_all(summed, "space", 0, 0, axis_index_groups=same_core, tiled=True)
    shares = pieces.astype(F32).sum(axis=0).astype(BF)
    spread = jnp.broadcast_to(shares[None], (levels, *shares.shape))
    grad_wo = lax.all_to_all(spread, "level", 0, 0, tiled=True).astype(F32).sum(axis=0)
    return (out_fields[None], grad_wo)


def solution(mesh):
    return jax.shard_map(
        body,
        mesh=mesh,
        in_specs=(
            P("level", "space", None),
            *([P()] * 12),
            P("space", None),
            P("space"),
            P("level", "space", None),
        ),
        out_specs=(P("level", "space", None), P("space", None)),
        check_vma=False,
    )
```

```python
import functools

import jax
import jax.numpy as jnp
from jax import lax
from jax.experimental import pallas as pl
from jax.experimental.pallas import tpu as pltpu
from jax.sharding import PartitionSpec as P

H = 12
HD = 64
PATCH = 256
PAIRS = H // 2
TEAM = 4
TEAMS = H // TEAM
GROUP = 16
LOG2E = 1.4426950408889634
epsilon = 1e-06
BF = jnp.bfloat16
F32 = jnp.float32
VMEM_BYTES = 24 * 1024 * 1024
MOST_VMEM = 63 * 1024 * 1024


def nn(a, b):
    return jnp.dot(a, b, preferred_element_type=F32)


def nt(a, b):
    return lax.dot_general(a, b, (((1,), (1,)), ((), ())), preferred_element_type=F32)


def normalize(values, gain):
    widened = values.astype(F32)
    mean_square = jnp.mean(widened * widened, axis=-1, keepdims=True)
    return (widened * lax.rsqrt(mean_square + epsilon) * gain).astype(BF)


def paired(queries):
    heads = queries.shape[0] // HD
    zero = jnp.zeros((HD, queries.shape[1]), BF)
    rows = []
    for head in range(heads):
        own = queries[head * HD : (head + 1) * HD]
        rows.append(jnp.concatenate([own if other == head else zero for other in range(heads)], axis=1))
    return jnp.concatenate(rows, axis=0)


def mixed(values, weights):
    ones = jnp.ones((16, values.shape[1]), BF)
    return nn(jnp.concatenate((values, ones), axis=0), weights)


def fetched(pairs, arrivals):
    copies = [pltpu.make_async_copy(a, b, arrivals.at[i]) for i, (a, b) in enumerate(pairs)]
    for copy in copies:
        copy.start()
    return copies


def turning_kernel(*refs):
    count = (len(refs) - 4) // 2
    ins, outs = refs[:count], refs[count : 2 * count]
    landed, turned, arrivals, sent = refs[2 * count :]
    copies = fetched([(ins[i], landed.at[i]) for i in range(count)], arrivals)
    stores = []
    for i in range(count):
        copies[i].wait()
        turned[i] = landed[i].T
        stores.append(pltpu.make_async_copy(turned.at[i], outs[i], sent.at[i]))
        stores[i].start()
    for store in stores:
        store.wait()


def vertical_kernel(
    _, x, wq_in, wk_in, wv_in, wo_in, gain, rows_of_bias, out, normed, q, k, v, mix, bias, wq, wk, wv, wo, arrivals
):
    levels, columns, features = x.shape
    copies = fetched([(wq_in, wq), (wk_in, wk), (wv_in, wv), (wo_in, wo)], arrivals)
    tokens = levels * columns
    block = levels * GROUP
    key_column = lax.broadcasted_iota(jnp.int32, (GROUP, TEAM * block), 0)
    query_column = lax.broadcasted_iota(jnp.int32, (GROUP, TEAM * block), 1) % GROUP
    same = key_column == query_column
    for team in range(TEAMS):
        for level in range(levels):
            row = rows_of_bias[team * levels + level : team * levels + level + 1]
            bias[team, level * GROUP : (level + 1) * GROUP] = jnp.where(same, row, -jnp.inf)
    for level in range(levels):
        rows = normalize(x[level], gain[...])
        for part in range(columns // GROUP):
            place = part * block + level * GROUP
            normed[place : place + GROUP] = rows[part * GROUP : (part + 1) * GROUP]
    spans = [slice(start, start + 256) for start in range(0, tokens, 256)]
    copies[0].wait()
    for span in spans:
        q[:, span] = (nt(wq[...], normed[span]) * (HD**-0.5 * LOG2E)).astype(BF)
    copies[1].wait()
    for span in spans:
        k[span] = nn(normed[span], wk[...]).astype(BF)
    copies[2].wait()
    for span in spans:
        v[:, span] = nt(wv[...], normed[span]).astype(BF)
    steps = [(part, team) for part in range(columns // GROUP) for team in range(TEAMS)]

    def step_scores(part, team):
        span, heads = slice(part * block, (part + 1) * block), slice(team * TEAM * HD, (team + 1) * TEAM * HD)
        return nn(k[span, heads], paired(q[heads, span])) + bias[team]

    def step_weights(scores, part, team):
        return jnp.exp2(scores - jnp.max(scores, axis=0, keepdims=True)).astype(BF)

    def step_mix(weights, part, team):
        span = slice(part * block, (part + 1) * block)
        for half in range(TEAM):
            head = slice((team * TEAM + half) * HD, (team * TEAM + half + 1) * HD)
            total = mixed(v[head, span], weights[:, half * block : (half + 1) * block])
            mix[head, span] = (total[:HD] / total[HD : HD + 1]).astype(BF)

    staged(steps, step_scores, step_weights, step_mix)
    copies[3].wait()
    for part in range(columns // GROUP):
        span = slice(part * block, (part + 1) * block)
        projected = nn(mix[:, span].T, wo[...])
        for level in range(levels):
            place = slice(part * GROUP, (part + 1) * GROUP)
            out[level, place] = (
                x[level, place].astype(F32) + projected[level * GROUP : (level + 1) * GROUP]
            ).astype(BF)


def pair_scores(pair, own, start, barred, q, k):
    heads = slice(pair * 128, (pair + 1) * 128)
    mine = slice(own * PATCH, (own + 1) * PATCH)
    return nn(k[pl.ds(start, PATCH), heads], paired(q[heads, mine]))


def pair_weights(scores, pair, own, start, barred, column, pbias, new, old):
    row = slice(own * PAIRS + pair, own * PAIRS + pair + 1)
    lane = lax.broadcasted_iota(jnp.int32, (1, 2 * PATCH), 1)
    bias = jnp.where(lane < PATCH, pbias[2 * pair, column], pbias[2 * pair + 1, column]) * LOG2E + barred
    largest = jnp.max(scores, axis=0, keepdims=True) + bias
    fade = None
    if old is not None:
        before = old[1][row]
        largest = jnp.maximum(before, largest)
        fade = jnp.exp2(before - largest)
    new[1][row] = largest
    return jnp.exp2(scores - (largest - bias)).astype(BF), fade


def absorb(weights, fade, pair, own, start, barred, v, new, old):
    mine = slice(own * PATCH, (own + 1) * PATCH)
    row = slice(own * PAIRS + pair, own * PAIRS + pair + 1)
    sums = []
    for half in range(2):
        head = slice(pair * 128 + half * HD, pair * 128 + half * HD + HD)
        part = slice(half * PATCH, (half + 1) * PATCH)
        found = mixed(v[head, pl.ds(start, PATCH)], weights[:, part])
        sums.append(found[HD : HD + 1])
        if old is None:
            new[0][head, mine] = found[:HD]
        else:
            new[0][head, mine] = old[0][head, mine] * fade[:, part] + found[:HD]
    both = jnp.concatenate(sums, axis=1)
    new[2][row] = both if old is None else old[2][row] * fade + both


def staged(steps, first, second, third):
    one, two = {}, {}
    for index in range(len(steps) + 2):
        if index < len(steps):
            one[index] = first(*steps[index])
        if 0 <= index - 1 < len(steps):
            two[index - 1] = second(one.pop(index - 1), *steps[index - 1])
        if 0 <= index - 2:
            third(two.pop(index - 2), *steps[index - 2])


def attend(places, column, q, k, v, pbias, new, old, project=None):
    def first(pair, own, start, barred):
        scores = pair_scores(pair, own, start, barred, q, k)
        if project is not None and own == places[0][0] and pair % 2 == 0 and pair + 2 < PAIRS:
            project(pair // 2 + 1)
        return scores

    if project is not None:
        project(0)
    staged(
        [(pair, *place) for place in places for pair in range(PAIRS)],
        first,
        lambda scores, *step: pair_weights(scores, *step, column, pbias, new, old),
        lambda found, *step: absorb(*found, *step, v, new, old),
    )


def keys_values(blocks, gain, wk, wv, k, v):
    pieces = [
        normalize(block[start : start + PATCH], gain[...])
        for block in blocks
        for start in range(0, block.shape[0], PATCH)
    ]

    def project(part):
        features = slice(part * 256, (part + 1) * 256)
        for index, piece in enumerate(pieces):
            span = slice(index * PATCH, (index + 1) * PATCH)
            v[features, span] = nt(wv[features], piece).astype(BF)
            k[span, features] = nn(piece, wk[:, features]).astype(BF)

    return project


def own_kernel(pbias, x, wq_in, wk_in, wv_in, gain, q, acc, top, total, wk, wv, again, k, v, wq, normed, arrivals):
    *loads, store = fetched([(wq_in, wq), (wk_in, wk), (wv_in, wv), (x, again)], arrivals)
    spans = [slice(start, start + PATCH) for start in range(0, x.shape[0], PATCH)]
    for span in spans:
        normed[span] = normalize(x[span], gain[...])
    loads[0].wait()
    for span in spans:
        q[:, span] = (nt(wq[...], normed[span]) * (HD**-0.5 * LOG2E)).astype(BF)
    loads[1].wait()
    for span in spans:
        k[span] = nn(normed[span], wk[...]).astype(BF)
    loads[2].wait()
    for span in spans:
        v[:, span] = nt(wv[...], normed[span]).astype(BF)
    attend([(0, 0, 0.0), (1, PATCH, 0.0)], 0, q, k, v, pbias, (acc, top, total), None)
    store.wait()


def arrived_part(distance, devices, place, near, live, pbias, blocks, gain, wk, wv, q, acc_in, top_in, total_in, acc, top, total, k, v):
    project = keys_values(blocks, gain, wk, wv, k, v)
    outwards = 1 - 2 * lax.rem(place[0], 2)
    source = lax.rem(place[0] + distance * outwards + devices, devices)
    places = []
    for own in range(2):
        found = jnp.int32(-1)
        for entry in range(near.shape[1]):
            listed = near[own, entry]
            hit = jnp.logical_and(entry < live[own], lax.shift_right_arithmetic(listed, 1) == source)
            found = jnp.where(hit, jnp.bitwise_and(listed, 1), found)
        barred = jnp.where(found >= 0, 0.0, -jnp.inf)
        places.append((own, pl.multiple_of(jnp.maximum(found, 0) * PATCH, PATCH), barred))
    attend(places, 1, q, k, v, pbias, (acc, top, total), (acc_in, top_in, total_in), project)


def arrived_kernel(distance, devices, count, place, near, live, pbias, *refs):
    blocks, (gain, wk, wv, q, *old) = refs[:count], refs[count : count + 7]
    new, (mark, k, v) = refs[count + 8 : count + 11], refs[count + 11 :]
    arrived_part(distance, devices, place, near, live, pbias, blocks, gain, wk, wv, q, *old, *new, k, v)
    mark[...] = new[2][:8, :128]


def last_kernel(
    distance, devices, place, near, live, pbias, x, gain, wk, wv, q, acc_in, top_in, total_in, cot_in, mix, keep, give,
    acc, top, total, k, v, cot, sent
):
    fetch = pltpu.make_async_copy(cot_in, cot, sent)
    fetch.start()
    old, new = (acc_in, top_in, total_in), (acc, top, total)
    arrived_part(distance, devices, place, near, live, pbias, (x,), gain, wk, wv, q, *old, *new, k, v)
    for pair in range(PAIRS):
        for own in range(2):
            mine = slice(own * PATCH, (own + 1) * PATCH)
            inverse = 1.0 / total[own * PAIRS + pair : own * PAIRS + pair + 1]
            for half in range(2):
                head = slice(pair * 128 + half * HD, pair * 128 + half * HD + HD)
                mix[head, mine] = (
                    acc[head, mine] * inverse[:, half * PATCH : (half + 1) * PATCH]
                ).astype(BF)
    fetch.wait()
    chips, rows, _ = keep.shape
    even = lax.rem(place[0], 2) == 0
    for first in range(0, chips, 8):
        span = slice(first * 2 * rows, (first + 8) * 2 * rows)
        grad = nn(mix[span], cot[...])
        for chip in range(8):
            at = chip * 2 * rows
            to_even, to_odd = grad[at : at + rows], grad[at + rows : at + 2 * rows]
            keep[first + chip] = jnp.where(even, to_even, to_odd)
            give[first + chip] = jnp.where(even, to_odd, to_even).astype(BF)


IN_VMEM = pl.BlockSpec(memory_space=pltpu.VMEM)
IN_SMEM = pl.BlockSpec(memory_space=pltpu.SMEM)
IN_HBM = pl.BlockSpec(memory_space=pltpu.HBM)


def kept_in_hbm(*arrays):
    return [pltpu.with_memory_space_constraint(array, pltpu.HBM) for array in arrays]


def turned(*arrays):
    shape = arrays[0].shape
    several = (len(arrays), *shape)
    return pl.pallas_call(
        turning_kernel,
        out_shape=[jax.ShapeDtypeStruct(shape, BF)] * len(arrays),
        in_specs=[IN_HBM] * len(arrays),
        out_specs=[IN_HBM] * len(arrays),
        scratch_shapes=[
            pltpu.VMEM(several, BF),
            pltpu.VMEM(several, BF),
            pltpu.SemaphoreType.DMA((len(arrays),)),
            pltpu.SemaphoreType.DMA((len(arrays),)),
        ],
        compiler_params=pltpu.CompilerParams(vmem_limit_bytes=MOST_VMEM),
        cost_estimate=pl.CostEstimate(flops=0, bytes_accessed=20 * 2**20, transcendentals=0),
        name="turned",
    )(*arrays)


def call(kernel, scalars, arrays, outs, scratch, flops, name, loose_in=(), loose_out=(), vmem=VMEM_BYTES):
    shapes = [jax.ShapeDtypeStruct(shape, kind) for shape, kind in outs]
    moved = flops // 256
    return pl.pallas_call(
        kernel,
        out_shape=shapes,
        in_specs=[IN_SMEM] * len(scalars) + [IN_HBM if i in loose_in else IN_VMEM for i in range(len(arrays))],
        out_specs=[IN_HBM if i in loose_out else IN_VMEM for i in range(len(outs))],
        scratch_shapes=[pltpu.VMEM(*s) if isinstance(s, tuple) else s for s in scratch],
        compiler_params=pltpu.CompilerParams(vmem_limit_bytes=vmem),
        cost_estimate=pl.CostEstimate(flops=flops, bytes_accessed=moved, transcendentals=0),
        name=name,
    )(*scalars, *arrays)


def halving_kernel(block, _, first, second, sent):
    rows = first.shape[0]
    for copy in fetched([(block.at[:rows], first), (block.at[rows:], second)], sent):
        copy.wait()


def halved(block, after):
    half = ((block.shape[0] // 2, block.shape[1]), BF)
    return call(
        halving_kernel,
        [],
        [block, after],
        [half, half],
        [pltpu.SemaphoreType.DMA((2,))],
        0,
        "halved",
        loose_in=(0, 1),
        loose_out=(0, 1),
    )


def expanded_bias(level_bias):
    levels = level_bias.shape[1]
    table = (level_bias * LOG2E).reshape(TEAMS, TEAM, levels, levels).transpose(0, 3, 1, 2)
    return jnp.repeat(table.reshape(TEAMS * levels, TEAM * levels), GROUP, axis=1)


MARK = ((8, 128), F32)


def sizes(columns, features):
    weights = ((features, features), BF)
    turned_tokens = ((features, columns), BF)
    state = [((features, columns), F32), ((2 * PAIRS, 2 * PATCH), F32), ((2 * PAIRS, 2 * PATCH), F32)]
    return weights, turned_tokens, ((columns, features), BF), state, columns * features * features


def run_vertical(place, x, wq, wk, wv, wo, gain, rows_of_bias):
    levels, share, features = x.shape
    weights, wide, tall, _, work = sizes(levels * share, features)
    return call(
        vertical_kernel,
        [place],
        [x, wq, wk, wv, wo, gain, rows_of_bias],
        [(x.shape, BF)],
        [
            tall,
            wide,
            tall,
            wide,
            wide,
            ((TEAMS, levels * GROUP, TEAM * levels * GROUP), F32),
            *([weights] * 4),
            pltpu.SemaphoreType.DMA((4,)),
        ],
        10 * work,
        "vertical",
        loose_in=range(1, 5),
    )[0]


def run_own(pbias, hidden, wq, wk, wv, gain):
    weights, wide, tall, state, work = sizes(*hidden.shape)
    return call(
        own_kernel,
        [pbias],
        [hidden, wq, wk, wv, gain],
        [wide, *state, weights, weights, tall],
        [tall, wide, weights, tall, pltpu.SemaphoreType.DMA((4,))],
        8 * work,
        "own",
        loose_in=(1, 2, 3),
        loose_out=(6,),
    )


def run_arrived(distance, devices, fixed, blocks, gain, wk, wv, q, state, after):
    _, wide, tall, kept, work = sizes(*q.shape[::-1])
    return call(
        functools.partial(arrived_kernel, distance, devices, len(blocks)),
        fixed,
        [*blocks, gain, wk, wv, q, *state, after],
        [*kept, MARK],
        [tall, wide],
        work // 4,
        "arrived",
        loose_in=(len(blocks) + 7,),
    )


def run_last(distance, devices, fixed, block, gain, wk, wv, q, state, cotangent):
    chips = devices // 2
    rows = block.shape[1] // (2 * chips)
    piece = (chips, rows, block.shape[1])
    _, wide, tall, kept, work = sizes(*block.shape)
    return call(
        functools.partial(last_kernel, distance, devices),
        fixed,
        [block, gain, wk, wv, q, *state, cotangent],
        [wide, (piece, F32), (piece, BF)],
        [*kept, tall, wide, tall, pltpu.SemaphoreType.DMA],
        8 * work,
        "last",
        loose_in=(8,),
    )


def body(
    fields,
    norm_vert,
    query_vert,
    keys_vert,
    values_vert,
    out_vert,
    level_bias,
    norm_patch,
    query_patch,
    keys_patch,
    values_patch,
    out_patch,
    patch_bias,
    neighbours,
    counts,
    cotangent,
):
    _, columns, features = fields.shape
    levels = lax.axis_size("level")
    devices = lax.axis_size("space")
    place = lax.axis_index("space")[None]
    share = columns // levels

    def moved(value, source_of):
        return lax.ppermute(value, "space", [(source_of(d) % devices, d) for d in range(devices)])

    wq_v, wv_v, wq_p, wv_p = kept_in_hbm(*turned(query_vert, values_vert, query_patch, values_patch))
    keys_vert, out_vert, keys_patch = kept_in_hbm(keys_vert, out_vert, keys_patch)
    x = lax.all_to_all(fields.reshape(levels, share, features), "level", 0, 0, tiled=True)
    hidden = run_vertical(place, x, wq_v, keys_vert, wv_v, out_vert, norm_vert[None], expanded_bias(level_bias))
    hidden = lax.all_to_all(hidden, "level", 0, 0, tiled=True).reshape(columns, features)

    def outer(d):
        return d + 2 if d % 2 == 0 else d - 2

    def inner(d):
        return d - 2 if d % 2 == 0 else d + 2

    def twin(d):
        return d ^ 1

    from_outer = moved(hidden, outer)
    from_twin = moved(hidden, twin)
    gain = norm_patch[None]
    q, *state, wk, wv, again = run_own(patch_bias, hidden, wq_p, keys_patch, wv_p, gain)
    from_inner = moved(again, inner)
    fixed = [place, neighbours, counts, patch_bias]
    *state, mark = run_arrived(1, devices, fixed, [from_twin], gain, wk, wv, q, state, jnp.zeros(*MARK))
    passed_on = [moved(half, twin) for half in halved(from_outer, mark)]
    *state, mark = run_arrived(2, devices, fixed, [from_outer], gain, wk, wv, q, state, mark)
    *state, _ = run_arrived(-1, devices, fixed, passed_on, gain, wk, wv, q, state, mark)
    mix, keep, give = run_last(
        -2, devices, fixed, from_inner, gain, wk, wv, q, state, *kept_in_hbm(cotangent.reshape(columns, features))
    )
    received = moved(give, twin)
    projected = lax.dot_general(mix, out_patch, (((0,), (0,)), ((), ())), preferred_element_type=F32)
    out_fields = (hidden.astype(F32) + projected).astype(BF)
    received, out_fields = lax.optimization_barrier((received, out_fields))
    summed = (keep + received.astype(F32)).astype(BF)
    same_core = [list(range(core, devices, 2)) for core in range(2)]
    pieces = lax.all_to_all(summed, "space", 0, 0, axis_index_groups=same_core, tiled=True)
    shares = pieces.astype(F32).sum(axis=0).astype(BF)
    spread = jnp.broadcast_to(shares[None], (levels, *shares.shape))
    grad_wo = lax.all_to_all(spread, "level", 0, 0, tiled=True).astype(F32).sum(axis=0)
    return (out_fields[None], grad_wo)


def solution(mesh):
    return jax.shard_map(
        body,
        mesh=mesh,
        in_specs=(
            P("level", "space", None),
            *([P()] * 12),
            P("space", None),
            P("space"),
            P("level", "space", None),
        ),
        out_specs=(P("level", "space", None), P("space", None)),
        check_vma=False,
    )
```

```python
import functools

import jax
import jax.numpy as jnp
from jax import lax
from jax.experimental import pallas as pl
from jax.experimental.pallas import tpu as pltpu
from jax.sharding import PartitionSpec as P

H = 12
HD = 64
PATCH = 256
PAIRS = H // 2
TEAM = 4
TEAMS = H // TEAM
GROUP = 16
LOG2E = 1.4426950408889634
epsilon = 1e-06
BF = jnp.bfloat16
F32 = jnp.float32
VMEM_BYTES = 24 * 1024 * 1024
MOST_VMEM = 63 * 1024 * 1024


def nn(a, b):
    return jnp.dot(a, b, preferred_element_type=F32)


def nt(a, b):
    return lax.dot_general(a, b, (((1,), (1,)), ((), ())), preferred_element_type=F32)


def normalize(values, gain):
    widened = values.astype(F32)
    mean_square = jnp.mean(widened * widened, axis=-1, keepdims=True)
    return (widened * lax.rsqrt(mean_square + epsilon) * gain).astype(BF)


def paired(queries):
    heads = queries.shape[0] // HD
    zero = jnp.zeros((HD, queries.shape[1]), BF)
    rows = []
    for head in range(heads):
        own = queries[head * HD : (head + 1) * HD]
        rows.append(jnp.concatenate([own if other == head else zero for other in range(heads)], axis=1))
    return jnp.concatenate(rows, axis=0)


def mixed(values, weights):
    ones = jnp.ones((16, values.shape[1]), BF)
    return nn(jnp.concatenate((values, ones), axis=0), weights)


def fetched(pairs, arrivals):
    copies = [pltpu.make_async_copy(a, b, arrivals.at[i]) for i, (a, b) in enumerate(pairs)]
    for copy in copies:
        copy.start()
    return copies


def turning_kernel(*refs):
    count = (len(refs) - 4) // 2
    ins, outs = refs[:count], refs[count : 2 * count]
    landed, turned, arrivals, sent = refs[2 * count :]
    copies = fetched([(ins[i], landed.at[i]) for i in range(count)], arrivals)
    stores = []
    for i in range(count):
        copies[i].wait()
        turned[i] = landed[i].T
        stores.append(pltpu.make_async_copy(turned.at[i], outs[i], sent.at[i]))
        stores[i].start()
    for store in stores:
        store.wait()


def vertical_kernel(
    _, _bias, x, wq_in, wk_in, wv_in, wo_in, gain, rows_of_bias, _gain, out, normed, q, k, v, mix, bias, wq, wk, wv, wo, arrivals
):
    levels, columns, features = x.shape
    copies = fetched([(wq_in, wq), (wk_in, wk), (wv_in, wv), (wo_in, wo)], arrivals)
    tokens = levels * columns
    block = levels * GROUP
    key_column = lax.broadcasted_iota(jnp.int32, (GROUP, TEAM * block), 0)
    query_column = lax.broadcasted_iota(jnp.int32, (GROUP, TEAM * block), 1) % GROUP
    same = key_column == query_column
    for team in range(TEAMS):
        for level in range(levels):
            row = rows_of_bias[team * levels + level : team * levels + level + 1]
            bias[team, level * GROUP : (level + 1) * GROUP] = jnp.where(same, row, -jnp.inf)
    for level in range(levels):
        rows = normalize(x[level], gain[...])
        for part in range(columns // GROUP):
            place = part * block + level * GROUP
            normed[place : place + GROUP] = rows[part * GROUP : (part + 1) * GROUP]
    spans = [slice(start, start + 256) for start in range(0, tokens, 256)]
    copies[0].wait()
    for span in spans:
        q[:, span] = (nt(wq[...], normed[span]) * (HD**-0.5 * LOG2E)).astype(BF)
    copies[1].wait()
    for span in spans:
        k[span] = nn(normed[span], wk[...]).astype(BF)
    copies[2].wait()
    for span in spans:
        v[:, span] = nt(wv[...], normed[span]).astype(BF)
    steps = [(part, team) for part in range(columns // GROUP) for team in range(TEAMS)]

    def step_scores(part, team):
        span, heads = slice(part * block, (part + 1) * block), slice(team * TEAM * HD, (team + 1) * TEAM * HD)
        return nn(k[span, heads], paired(q[heads, span])) + bias[team]

    def step_weights(scores, part, team):
        return jnp.exp2(scores - jnp.max(scores, axis=0, keepdims=True)).astype(BF)

    def step_mix(weights, part, team):
        span = slice(part * block, (part + 1) * block)
        for half in range(TEAM):
            head = slice((team * TEAM + half) * HD, (team * TEAM + half + 1) * HD)
            total = mixed(v[head, span], weights[:, half * block : (half + 1) * block])
            mix[head, span] = (total[:HD] / total[HD : HD + 1]).astype(BF)

    staged(steps, step_scores, step_weights, step_mix)
    copies[3].wait()
    for part in range(columns // GROUP):
        span = slice(part * block, (part + 1) * block)
        projected = nn(mix[:, span].T, wo[...])
        for level in range(levels):
            place = slice(part * GROUP, (part + 1) * GROUP)
            out[level, place] = (
                x[level, place].astype(F32) + projected[level * GROUP : (level + 1) * GROUP]
            ).astype(BF)


def pair_scores(pair, own, start, barred, q, k):
    heads = slice(pair * 128, (pair + 1) * 128)
    mine = slice(own * PATCH, (own + 1) * PATCH)
    return nn(k[pl.ds(start, PATCH), heads], paired(q[heads, mine]))


def pair_weights(scores, pair, own, start, barred, column, pbias, new, old):
    row = slice(own * PAIRS + pair, own * PAIRS + pair + 1)
    lane = lax.broadcasted_iota(jnp.int32, (1, 2 * PATCH), 1)
    bias = jnp.where(lane < PATCH, pbias[2 * pair, column], pbias[2 * pair + 1, column]) * LOG2E + barred
    largest = jnp.max(scores, axis=0, keepdims=True) + bias
    fade = None
    if old is not None:
        before = old[1][row]
        largest = jnp.maximum(before, largest)
        fade = jnp.exp2(before - largest)
    new[1][row] = largest
    return jnp.exp2(scores - (largest - bias)).astype(BF), fade


def absorb(weights, fade, pair, own, start, barred, v, new, old):
    mine = slice(own * PATCH, (own + 1) * PATCH)
    row = slice(own * PAIRS + pair, own * PAIRS + pair + 1)
    sums = []
    for half in range(2):
        head = slice(pair * 128 + half * HD, pair * 128 + half * HD + HD)
        part = slice(half * PATCH, (half + 1) * PATCH)
        found = mixed(v[head, pl.ds(start, PATCH)], weights[:, part])
        sums.append(found[HD : HD + 1])
        if old is None:
            new[0][head, mine] = found[:HD]
        else:
            new[0][head, mine] = old[0][head, mine] * fade[:, part] + found[:HD]
    both = jnp.concatenate(sums, axis=1)
    new[2][row] = both if old is None else old[2][row] * fade + both


def staged(steps, first, second, third):
    one, two = {}, {}
    for index in range(len(steps) + 2):
        if index < len(steps):
            one[index] = first(*steps[index])
        if 0 <= index - 1 < len(steps):
            two[index - 1] = second(one.pop(index - 1), *steps[index - 1])
        if 0 <= index - 2:
            third(two.pop(index - 2), *steps[index - 2])


def attend(places, column, q, k, v, pbias, new, old):
    staged(
        [(pair, *place) for place in places for pair in range(PAIRS)],
        lambda *step: pair_scores(*step, q, k),
        lambda scores, *step: pair_weights(scores, *step, column, pbias, new, old),
        lambda found, *step: absorb(*found, *step, v, new, old),
    )


def keys_values(blocks, gain, wk, wv, k, v):
    done = 0
    for block in blocks:
        for start in range(0, block.shape[0], PATCH):
            span = slice(done, done + PATCH)
            piece = normalize(block[start : start + PATCH], gain[...])
            v[:, span] = nt(wv[...], piece).astype(BF)
            k[span] = nn(piece, wk[...]).astype(BF)
            done += PATCH


def own_kernel(pbias, x, wq_in, wk_in, wv_in, gain, q, acc, top, total, wk, wv, again, k, v, wq, normed, arrivals):
    *loads, store = fetched([(wq_in, wq), (wk_in, wk), (wv_in, wv), (x, again)], arrivals)
    spans = [slice(start, start + PATCH) for start in range(0, x.shape[0], PATCH)]
    for span in spans:
        normed[span] = normalize(x[span], gain[...])
    loads[0].wait()
    for span in spans:
        q[:, span] = (nt(wq[...], normed[span]) * (HD**-0.5 * LOG2E)).astype(BF)
    loads[1].wait()
    for span in spans:
        k[span] = nn(normed[span], wk[...]).astype(BF)
    loads[2].wait()
    for span in spans:
        v[:, span] = nt(wv[...], normed[span]).astype(BF)
    attend([(0, 0, 0.0), (1, PATCH, 0.0)], 0, q, k, v, pbias, (acc, top, total), None)
    store.wait()


def arrived_part(distance, devices, place, near, live, pbias, blocks, gain, wk, wv, q, acc_in, top_in, total_in, acc, top, total, k, v):
    keys_values(blocks, gain, wk, wv, k, v)
    outwards = 1 - 2 * lax.rem(place[0], 2)
    source = lax.rem(place[0] + distance * outwards + devices, devices)
    places = []
    for own in range(2):
        found = jnp.int32(-1)
        for entry in range(near.shape[1]):
            listed = near[own, entry]
            hit = jnp.logical_and(entry < live[own], lax.shift_right_arithmetic(listed, 1) == source)
            found = jnp.where(hit, jnp.bitwise_and(listed, 1), found)
        barred = jnp.where(found >= 0, 0.0, -jnp.inf)
        places.append((own, pl.multiple_of(jnp.maximum(found, 0) * PATCH, PATCH), barred))
    attend(places, 1, q, k, v, pbias, (acc, top, total), (acc_in, top_in, total_in))


def arrived_kernel(distance, devices, count, place, near, live, pbias, *refs):
    blocks, (gain, wk, wv, q, *old) = refs[:count], refs[count : count + 7]
    new, (mark, k, v) = refs[count + 8 : count + 11], refs[count + 11 :]
    arrived_part(distance, devices, place, near, live, pbias, blocks, gain, wk, wv, q, *old, *new, k, v)
    mark[...] = new[2][:8, :128]


def last_kernel(
    distance, devices, place, near, live, pbias, x, gain, wk, wv, q, acc_in, top_in, total_in, cot_in, mix_out, keep, give,
    acc, top, total, k, v, mix, cot, sent
):
    fetch = pltpu.make_async_copy(cot_in, cot, sent.at[0])
    fetch.start()
    old, new = (acc_in, top_in, total_in), (acc, top, total)
    arrived_part(distance, devices, place, near, live, pbias, (x,), gain, wk, wv, q, *old, *new, k, v)
    for pair in range(PAIRS):
        for own in range(2):
            mine = slice(own * PATCH, (own + 1) * PATCH)
            inverse = 1.0 / total[own * PAIRS + pair : own * PAIRS + pair + 1]
            for half in range(2):
                head = slice(pair * 128 + half * HD, pair * 128 + half * HD + HD)
                mix[head, mine] = (
                    acc[head, mine] * inverse[:, half * PATCH : (half + 1) * PATCH]
                ).astype(BF)
    store = pltpu.make_async_copy(mix, mix_out, sent.at[1])
    store.start()
    fetch.wait()
    chips, rows, _ = keep.shape
    even = lax.rem(place[0], 2) == 0
    for first in range(0, chips, 8):
        span = slice(first * 2 * rows, (first + 8) * 2 * rows)
        grad = nn(mix[span], cot[...])
        for chip in range(8):
            at = chip * 2 * rows
            to_even, to_odd = grad[at : at + rows], grad[at + rows : at + 2 * rows]
            keep[first + chip] = jnp.where(even, to_even, to_odd)
            give[first + chip] = jnp.where(even, to_odd, to_even).astype(BF)
    store.wait()


IN_VMEM = pl.BlockSpec(memory_space=pltpu.VMEM)
IN_SMEM = pl.BlockSpec(memory_space=pltpu.SMEM)
IN_HBM = pl.BlockSpec(memory_space=pltpu.HBM)


def kept_in_hbm(*arrays):
    return [pltpu.with_memory_space_constraint(array, pltpu.HBM) for array in arrays]


def turned(*arrays):
    shape = arrays[0].shape
    several = (len(arrays), *shape)
    return pl.pallas_call(
        turning_kernel,
        out_shape=[jax.ShapeDtypeStruct(shape, BF)] * len(arrays),
        in_specs=[IN_HBM] * len(arrays),
        out_specs=[IN_HBM] * len(arrays),
        scratch_shapes=[
            pltpu.VMEM(several, BF),
            pltpu.VMEM(several, BF),
            pltpu.SemaphoreType.DMA((len(arrays),)),
            pltpu.SemaphoreType.DMA((len(arrays),)),
        ],
        compiler_params=pltpu.CompilerParams(vmem_limit_bytes=MOST_VMEM),
        cost_estimate=pl.CostEstimate(flops=0, bytes_accessed=20 * 2**20, transcendentals=0),
        name="turned",
    )(*arrays)


def call(kernel, scalars, arrays, outs, scratch, flops, name, loose_in=(), loose_out=(), vmem=VMEM_BYTES):
    shapes = [jax.ShapeDtypeStruct(shape, kind) for shape, kind in outs]
    moved = flops // 256
    return pl.pallas_call(
        kernel,
        out_shape=shapes,
        in_specs=[IN_SMEM] * len(scalars) + [IN_HBM if i in loose_in else IN_VMEM for i in range(len(arrays))],
        out_specs=[IN_HBM if i in loose_out else IN_VMEM for i in range(len(outs))],
        scratch_shapes=[pltpu.VMEM(*s) if isinstance(s, tuple) else s for s in scratch],
        compiler_params=pltpu.CompilerParams(vmem_limit_bytes=vmem),
        cost_estimate=pl.CostEstimate(flops=flops, bytes_accessed=moved, transcendentals=0),
        name=name,
    )(*scalars, *arrays)


def halving_kernel(block, _, first, second, sent):
    rows = first.shape[0]
    for copy in fetched([(block.at[:rows], first), (block.at[rows:], second)], sent):
        copy.wait()


def halved(block, after):
    half = ((block.shape[0] // 2, block.shape[1]), BF)
    return call(
        halving_kernel,
        [],
        [block, after],
        [half, half],
        [pltpu.SemaphoreType.DMA((2,))],
        0,
        "halved",
        loose_in=(0, 1),
        loose_out=(0, 1),
    )


def expanded_bias(level_bias):
    levels = level_bias.shape[1]
    table = (level_bias * LOG2E).reshape(TEAMS, TEAM, levels, levels).transpose(0, 3, 1, 2)
    return jnp.repeat(table.reshape(TEAMS * levels, TEAM * levels), GROUP, axis=1)


MARK = ((8, 128), F32)


def sizes(columns, features):
    weights = ((features, features), BF)
    turned_tokens = ((features, columns), BF)
    state = [((features, columns), F32), ((2 * PAIRS, 2 * PATCH), F32), ((2 * PAIRS, 2 * PATCH), F32)]
    return weights, turned_tokens, ((columns, features), BF), state, columns * features * features


def run_vertical(early, x, wq, wk, wv, wo, gain, rows_of_bias, later_gain):
    levels, share, features = x.shape
    weights, wide, tall, _, work = sizes(levels * share, features)
    return call(
        vertical_kernel,
        early,
        [x, wq, wk, wv, wo, gain, rows_of_bias, later_gain],
        [(x.shape, BF)],
        [
            tall,
            wide,
            tall,
            wide,
            wide,
            ((TEAMS, levels * GROUP, TEAM * levels * GROUP), F32),
            *([weights] * 4),
            pltpu.SemaphoreType.DMA((4,)),
        ],
        10 * work,
        "vertical",
        loose_in=range(1, 5),
    )[0]


def run_own(pbias, hidden, wq, wk, wv, gain):
    weights, wide, tall, state, work = sizes(*hidden.shape)
    return call(
        own_kernel,
        [pbias],
        [hidden, wq, wk, wv, gain],
        [wide, *state, weights, weights, tall],
        [tall, wide, weights, tall, pltpu.SemaphoreType.DMA((4,))],
        8 * work,
        "own",
        loose_in=(1, 2, 3),
        loose_out=(6,),
    )


def run_arrived(distance, devices, fixed, blocks, gain, wk, wv, q, state, after):
    _, wide, tall, kept, work = sizes(*q.shape[::-1])
    return call(
        functools.partial(arrived_kernel, distance, devices, len(blocks)),
        fixed,
        [*blocks, gain, wk, wv, q, *state, after],
        [*kept, MARK],
        [tall, wide],
        work // 4,
        "arrived",
        loose_in=(len(blocks) + 7,),
    )


def run_last(distance, devices, fixed, block, gain, wk, wv, q, state, cotangent):
    chips = devices // 2
    rows = block.shape[1] // (2 * chips)
    piece = (chips, rows, block.shape[1])
    _, wide, tall, kept, work = sizes(*block.shape)
    return call(
        functools.partial(last_kernel, distance, devices),
        fixed,
        [block, gain, wk, wv, q, *state, cotangent],
        [wide, (piece, F32), (piece, BF)],
        [*kept, tall, wide, wide, tall, pltpu.SemaphoreType.DMA((2,))],
        8 * work,
        "last",
        loose_in=(8,),
        loose_out=(0,),
    )


def body(
    fields,
    norm_vert,
    query_vert,
    keys_vert,
    values_vert,
    out_vert,
    level_bias,
    norm_patch,
    query_patch,
    keys_patch,
    values_patch,
    out_patch,
    patch_bias,
    neighbours,
    counts,
    cotangent,
):
    _, columns, features = fields.shape
    levels = lax.axis_size("level")
    devices = lax.axis_size("space")
    place = lax.axis_index("space")[None]
    share = columns // levels

    def moved(value, source_of):
        return lax.ppermute(value, "space", [(source_of(d) % devices, d) for d in range(devices)])

    wq_v, wv_v, wq_p, wv_p = kept_in_hbm(*turned(query_vert, values_vert, query_patch, values_patch))
    keys_vert, out_vert, keys_patch = kept_in_hbm(keys_vert, out_vert, keys_patch)
    x = lax.all_to_all(fields.reshape(levels, share, features), "level", 0, 0, tiled=True)
    gain = norm_patch[None]
    hidden = run_vertical(
        [place, patch_bias], x, wq_v, keys_vert, wv_v, out_vert, norm_vert[None], expanded_bias(level_bias), gain
    )
    hidden = lax.all_to_all(hidden, "level", 0, 0, tiled=True).reshape(columns, features)

    def outer(d):
        return d + 2 if d % 2 == 0 else d - 2

    def inner(d):
        return d - 2 if d % 2 == 0 else d + 2

    def twin(d):
        return d ^ 1

    from_outer = moved(hidden, outer)
    from_twin = moved(hidden, twin)
    q, *state, wk, wv, again = run_own(patch_bias, hidden, wq_p, keys_patch, wv_p, gain)
    from_inner = moved(again, inner)
    fixed = [place, neighbours, counts, patch_bias]
    *state, mark = run_arrived(1, devices, fixed, [from_twin], gain, wk, wv, q, state, jnp.zeros(*MARK))
    passed_on = [moved(half, twin) for half in halved(from_outer, mark)]
    *state, mark = run_arrived(2, devices, fixed, [from_outer], gain, wk, wv, q, state, mark)
    *state, _ = run_arrived(-1, devices, fixed, passed_on, gain, wk, wv, q, state, mark)
    mix, keep, give = run_last(
        -2, devices, fixed, from_inner, gain, wk, wv, q, state, *kept_in_hbm(cotangent.reshape(columns, features))
    )
    received = moved(give, twin)
    projected = lax.dot_general(mix, out_patch, (((0,), (0,)), ((), ())), preferred_element_type=F32)
    out_fields = (hidden.astype(F32) + projected).astype(BF)
    received, out_fields = lax.optimization_barrier((received, out_fields))
    summed = (keep + received.astype(F32)).astype(BF)
    same_core = [list(range(core, devices, 2)) for core in range(2)]
    pieces = lax.all_to_all(summed, "space", 0, 0, axis_index_groups=same_core, tiled=True)
    shares = pieces.astype(F32).sum(axis=0).astype(BF)
    spread = jnp.broadcast_to(shares[None], (levels, *shares.shape))
    grad_wo = lax.all_to_all(spread, "level", 0, 0, tiled=True).astype(F32).sum(axis=0)
    return (out_fields[None], grad_wo)


def solution(mesh):
    return jax.shard_map(
        body,
        mesh=mesh,
        in_specs=(
            P("level", "space", None),
            *([P()] * 12),
            P("space", None),
            P("space"),
            P("level", "space", None),
        ),
        out_specs=(P("level", "space", None), P("space", None)),
        check_vma=False,
    )
```
